32 devices in a mesh: members: 2 (over y), belt: 4 (over z), across: 2 (over x), lev: 2 (over core).
Axes of the slice: x: 2, y: 2, z: 4, core: 2. Of those that a mesh axis runs over, the one named last changes fastest.
Arguments:
- wind: bfloat16 [2, 24, 64, 4096], P(None, ('members', 'lev'), 'across', 'belt'), parts along dimension 1, may hold values from -6 to 6
- metric: float32 [64, 4096], P('across', 'belt'), may hold values from 0.5 to 2
- kappa: float32 [2, 64, 4096], P(None, 'across', 'belt'), may hold values from 0.03 to 0.24
- edge_peer: int32 [2, 4], replicated, may hold values from 0 to 3, each once within a row
- edge_flip: int32 [2, 4], replicated, may hold values from 0 to 1
- edge_turn: int32 [2, 4], replicated, may hold values from 0 to 3
Outputs:
- controls: float32 [2, 24, 64, 4096], P(None, ('members', 'lev'), 'across', 'belt'), parts along dimension 1
The draws below stay inside these ranges and needn't reach their ends.
There are 2 independent parts, one for each index of `members`. The reference program is written for one: setup_inputs(seed, part) draws one part's arguments, and reference() takes and returns one part's arrays. A program takes and returns all parts, laid end to end along the dimension named above; an argument that names none is the same for every part. Nothing has to cross between parts.
Inputs may be any that keep to these rules, and one draw needn't show every extreme that they name: `edge_peer`: each row names every column block once.
All inputs are finite; a program needn't handle non-finite values.
Results may differ from the reference program's by a relative error of at most 0.0003.
Values may be sent and summed in bfloat16 or wider, within the bound.
No kernel may reach another device: no remote copies, remote signals or barrier semaphores. Data moves between devices by JAX's collectives and lax.ppermute only.
A program may use at most 64 MiB of HBM per device.

```python
import math
import jax
import jax.numpy as jnp
from jax import lax

CB = 1024
STEPS = 6
LEV = 12
NA = 64
NB = 4096
BLOCKS = 4


def set_ends(values, own_key, low, high):
    place = [jax.random.randint(jax.random.fold_in(own_key, axis), (), 0, length) for axis, length in enumerate(values.shape)]
    main_axis = values.shape.index(max(values.shape))
    beside = place[:main_axis] + [(place[main_axis] + 1) % values.shape[main_axis]] + place[main_axis + 1:]
    return values.at[tuple(place)].set(low).at[tuple(beside)].set(high)


def shard_levels(own_key, shape, pieces, low, high):
    factor_of, own = 1.0, jax.random.fold_in(own_key, 6)
    for axis_at, parts in pieces:
        steps = jnp.exp(jax.random.uniform(jax.random.fold_in(own, axis_at), (parts,), jnp.float32, low / len(pieces), high / len(pieces)))
        factor_of = factor_of * jnp.repeat(steps, shape[axis_at] // parts).reshape([-1 if axis == axis_at else 1 for axis in range(len(shape))])
    return factor_of


def bell_draw(key, extent, deviation, reach, shards=(), held_as=jnp.bfloat16):
    level = shard_levels(key, extent, shards, -0.22, 0.18) if shards else 1.0
    entries = jax.random.normal(key, extent, jnp.float32) * deviation * level
    return jnp.minimum(jnp.maximum(entries, -reach), reach).astype(held_as)


def setup_inputs(seed: int = 0, part: int = 0) -> dict:
    seeds = jax.random.split(jax.random.key(seed), 7)
    own_keys = jax.random.split(jax.random.fold_in(seeds[6], part), 7)
    wind = bell_draw(own_keys[0], (2, LEV, NA, NB), 1.0, 6.0, ((1, 2), (2, 2), (3, 4)))
    metric = jnp.clip(jnp.exp(math.log(2.0) - 1.3862944 * jax.random.uniform(seeds[1], (NA, NB), jnp.float32) ** shard_levels(seeds[1], (NA, NB), ((0, 2), (1, 4)), -0.2, 0.2)), 0.5, 2.0)
    kappa = jnp.clip(jnp.exp(math.log(0.24) - 2.0794415 * jax.random.uniform(seeds[2], (2, NA, NB), jnp.float32) ** shard_levels(seeds[2], (2, NA, NB), ((1, 2), (2, 4)), -0.2, 0.2)), 0.03, 0.24)
    edge_peer = jax.vmap(lambda own: jax.random.permutation(own, BLOCKS))(jax.random.split(seeds[3], 2)).reshape((2, BLOCKS)).astype(jnp.int32)
    edge_flip = set_ends(jax.random.randint(seeds[4], (2, BLOCKS), 0, 2), jax.random.fold_in(seeds[4], 1), 0, 1).astype(jnp.int32)
    edge_turn = set_ends(jax.random.randint(seeds[5], (2, BLOCKS), 0, 4), jax.random.fold_in(seeds[5], 1), 0, 3).astype(jnp.int32)
    return {"wind": wind, "metric": metric, "kappa": kappa, "edge_peer": edge_peer, "edge_flip": edge_flip, "edge_turn": edge_turn}


def turn_factors(turns):
    cosine = jnp.where(turns == 0, 1.0, jnp.where(turns == 2, -1.0, 0.0)).astype(jnp.float32)
    sine_neg = jnp.where(turns == 1, -1.0, jnp.where(turns == 3, 1.0, 0.0)).astype(jnp.float32)
    return cosine, sine_neg


def pole_row(rim_row, peers, flips, turns):
    column = jnp.arange(NB, dtype=jnp.int32)
    blocks = (column // CB).astype(jnp.int32)
    offset = (column % CB).astype(jnp.int32)
    source = peers[blocks] * CB + jnp.where(flips[blocks] == 1, CB - 1 - offset, offset)
    moved = rim_row[:, source]
    cosine, sine_neg = turn_factors(turns[blocks])
    eastward = cosine * moved[0] + sine_neg * moved[1]
    northward = cosine * moved[1] - sine_neg * moved[0]
    return jnp.stack([eastward, northward])


def diffuse(fields, belt_coef, across_coef):
    belt_flux = belt_coef * (jnp.roll(fields, -1, 2) - fields)
    across_flux = across_coef * (fields[:, 1:] - fields[:, :-1])
    border = jnp.zeros((fields.shape[0], 1, fields.shape[2]), jnp.float32)
    return fields + belt_flux - jnp.roll(belt_flux, 1, 2) + jnp.concatenate([across_flux, border], 1) - jnp.concatenate([border, across_flux], 1)


def reference(wind, metric, kappa, edge_peer, edge_flip, edge_turn):
    belt_coef = 0.5 * (kappa + jnp.roll(kappa, -1, 2))
    across_coef = 0.5 * (kappa[:, :-1] + kappa[:, 1:])

    def one_level(level_wind):
        winds = level_wind.astype(jnp.float32)
        north = pole_row(winds[:, 0, :], edge_peer[0], edge_flip[0], edge_turn[0])
        south = pole_row(winds[:, NA - 1, :], edge_peer[1], edge_flip[1], edge_turn[1])
        extended = jnp.concatenate([north[:, None], winds, south[:, None]], 1)
        across_diff = 0.5 * (extended[:, 2:] - extended[:, :-2])
        belt_diff = 0.5 * (jnp.roll(winds, -1, 2) - jnp.roll(winds, 1, 2))
        curl_part = metric * (across_diff[0] - belt_diff[1])
        divergent = metric * (-belt_diff[0] - across_diff[1])
        fields = jnp.stack([curl_part, divergent])
        for repeat in range(STEPS):
            fields = diffuse(fields, belt_coef, across_coef)
        return fields

    result = lax.map(one_level, jnp.moveaxis(wind, 1, 0))
    return jnp.moveaxis(result, 0, 1)
```

```python
import functools

import jax
import jax.numpy as jnp
from jax import lax
from jax.experimental import pallas as pl
from jax.experimental.pallas import tpu as pltpu
from jax.sharding import PartitionSpec as P

STEPS = 6
LANES = 128
SUB = 8
SLOTS = 8
BF = jnp.bfloat16
F32 = jnp.float32


def split_hi_lo(value):
    hi = value.astype(BF).astype(F32)
    return hi, value - hi


def lane_iota():
    return lax.broadcasted_iota(jnp.int32, (SUB, LANES), 1)


def sub_iota(width):
    return lax.broadcasted_iota(jnp.int32, (SUB, width), 0)


def compact(tiles):
    slot = lane_iota() // 16
    packed = []
    for at in range(0, len(tiles), SLOTS):
        total = None
        for g, tile in enumerate(tiles[at : at + SLOTS]):
            moved = pltpu.roll(tile, (8 + 16 * g) % LANES, 1)
            total = moved if total is None else jnp.where(slot == g, moved, total)
        packed.append(total)
    return packed


def expand(packed, index):
    tile = packed[index // SLOTS]
    return pltpu.roll(tile, (-(8 + 16 * (index % SLOTS))) % LANES, 1)


def pack_kernel(ends, place_ref, wind_ref, metric_ref, kappa_ref, bulk_ref, corner_ref, side_ref, rim_ref):
    fields, levels, rows, cols = (2, wind_ref.shape[1], wind_ref.shape[2], wind_ref.shape[3])
    first = place_ref[1] == 0
    left = lane_iota() < LANES // 2
    top, bottom = slice(0, SUB), slice(rows - SUB, rows)

    def bands(whole):
        if ends == "pick":
            return [jnp.where(first, whole[bottom], whole[top])]
        return [whole[bottom], whole[top]]

    def edge(band):
        return jnp.where(left, band[:, :LANES], band[:, cols - LANES :])

    counts = 1 if ends == "pick" else 2
    band_rows = [[] for _ in range(counts)]
    side_tiles = []
    rim_rows = []
    for c in range(fields):
        for lev in range(levels):
            whole = wind_ref[c, lev].astype(F32)
            for at, band in enumerate(bands(whole)):
                band_rows[at].append(band)
            side_tiles += [edge(whole[r : r + SUB]) for r in range(0, rows, SUB)]
            rim_rows.append(jnp.where(first, whole[0:1], whole[rows - 1 : rows]))
    for q in range(fields + 1):
        whole = kappa_ref[q] if q < fields else metric_ref[...]
        for part in split_hi_lo(whole):
            for at, band in enumerate(bands(part)):
                band_rows[at].append(band)
            side_tiles += [edge(part[r : r + SUB]) for r in range(0, rows, SUB)]
    for at in range(counts):
        pieces = band_rows[at]
        for i in range(0, len(pieces), 2):
            both = jnp.concatenate([pieces[i], pieces[i + 1]], axis=0)
            bulk_ref[at, SUB * i : SUB * (i + 2)] = both.astype(BF)
        packed = compact([edge(p) for p in pieces])
        packed += [jnp.zeros((SUB, LANES), F32)] * (-len(packed) % 2)
        corner_ref[at] = jnp.concatenate(packed, axis=0).astype(BF)
    packed = compact(side_tiles)
    packed += [jnp.zeros((SUB, LANES), F32)] * (-len(packed) % 2)
    rim = jnp.concatenate(rim_rows + [jnp.zeros((16 - len(rim_rows), cols), F32)], axis=0).astype(BF)
    rim_ref[...] = rim
    side_ref[0:16] = rim
    for i in range(0, len(packed), 2):
        both = jnp.concatenate(packed[i : i + 2], axis=0).astype(BF)
        side_ref[16:32, LANES * (i // 2) : LANES * (i // 2 + 1)] = both
    done = LANES * (len(packed) // 2)
    side_ref[16:32, done:] = jnp.zeros((16, cols - done), BF)


def main_kernel(
    halves, slots, place_ref, wind_ref, metric_ref, kappa_ref, bulk_ref, side_a_ref, side_b_ref,
    corner_a_ref, corner_b_ref, rims_ref, out_ref, km_ref, coef_ref, ghost_ref,
):
    levels, rows, cols = wind_ref.shape[1], wind_ref.shape[2], wind_ref.shape[3]
    width = cols + LANES
    height = rows + SUB * halves
    tiles = rows // SUB
    at_belt, at_across, n_across = place_ref[0], place_ref[1], place_ref[2]
    first, last = at_across == 0, at_across == n_across - 1
    left = lane_iota() < LANES // 2
    even = lax.rem(at_belt, 2) == 0

    def side_tile(index):
        at, column = 16 + SUB * ((index // SLOTS) % 2), LANES * (index // SLOTS // 2)
        a = side_a_ref[16:32, column : column + LANES].astype(F32)[at - 16 : at - 8]
        b = side_b_ref[16:32, column : column + LANES].astype(F32)[at - 16 : at - 8]
        both = jnp.where(left == even, a, b)
        return pltpu.roll(both, (-(8 + 16 * (index % SLOTS))) % LANES, 1)

    def mix(index, a, b):
        shift = (-(8 + 16 * (index % SLOTS))) % LANES
        a = pltpu.roll(a, shift, 1)
        b = pltpu.roll(b, shift, 1)
        return jnp.where(left == even, a, b)

    def own_halo(index):
        group = index // SLOTS
        column = LANES * (group // 2)
        half = slice(SUB * (group % 2), SUB * (group % 2) + SUB)
        a = side_a_ref[16:32, column : column + LANES].astype(F32)[half]
        b = side_b_ref[16:32, column : column + LANES].astype(F32)[half]
        return mix(index, a, b)

    def band_halo(at, index):
        group = index // SLOTS
        base = 16 * (group // 2)
        half = slice(SUB * (group % 2), SUB * (group % 2) + SUB)
        a = corner_a_ref[at, base : base + 16].astype(F32)[half]
        b = corner_b_ref[at, base : base + 16].astype(F32)[half]
        return mix(index, a, b)

    def band(at, index):
        base = 16 * (index // 2)
        half = slice(SUB * (index % 2), SUB * (index % 2) + SUB)
        body = bulk_ref[at, base : base + 16].astype(F32)[half]
        return jnp.concatenate([body, band_halo(at, index)], axis=1)

    def slab(own, index, piece):
        halo = jnp.concatenate([own_halo(index * tiles + r) for r in range(tiles)], axis=0)
        rows_own = jnp.concatenate([own, halo], axis=1)
        return jnp.concatenate([rows_own] + [piece(at) for at in range(halves)], axis=0)

    @pl.when(pl.program_id(0) == 0)
    def _():
        fields = 2 * levels
        for q in range(3):
            own = kappa_ref[q] if q < 2 else metric_ref[...]
            hi, lo = split_hi_lo(own)
            i = fields + 2 * q
            km_ref[q] = slab(hi, i, lambda at, i=i: band(at, i)) + slab(
                lo, i + 1, lambda at, i=i: band(at, i + 1)
            )
        at_row = lax.broadcasted_iota(jnp.int32, (height, width), 0)
        closed = ((at_row == rows - 1) & last) | ((at_row == height - 1) & first)
        for q in range(2):
            kappa = km_ref[q]
            east = 0.5 * (kappa + pltpu.roll(kappa, width - 1, 1))
            west = pltpu.roll(east, 1, 1)
            south = jnp.where(closed, 0.0, 0.5 * (kappa + pltpu.roll(kappa, height - 1, 0)))
            north = pltpu.roll(south, 1, 0)
            coef_ref[q, 0] = 1.0 - ((east + west) + (south + north))
            coef_ref[q, 1] = east
            coef_ref[q, 2] = west
            coef_ref[q, 3] = south
            coef_ref[q, 4] = north
        km_ref[2] = 0.5 * km_ref[2]
        edge = jnp.where(first, 0, 1)
        n_belt = place_ref[3]
        lane_r = lax.broadcasted_iota(jnp.int32, (LANES, LANES), 0)
        lane_c = lax.broadcasted_iota(jnp.int32, (LANES, LANES), 1)
        forward = jnp.where(lane_r == lane_c, 1.0, 0.0)
        backward = jnp.where(lane_r + lane_c == LANES - 1, 1.0, 0.0)

        def ghost_tile(block, t):
            base = 4 + 3 * (edge * n_belt + block)
            peer, flip, turn = place_ref[base], place_ref[base + 1], place_ref[base + 2]
            flipped = flip == 1
            source = jnp.where(flipped, cols // LANES - 1 - t, t)
            found = None
            slot = place_ref[4 + 6 * n_belt + peer]
            raw = rims_ref[slot, :, pl.ds(pl.multiple_of(source * LANES, LANES), LANES)]
            turned = jnp.where(flipped, backward, forward).astype(BF)
            found = jnp.dot(raw, turned, preferred_element_type=F32)
            p, q = found[0:levels], found[levels : 2 * levels]
            cosine = jnp.where(turn == 0, 1.0, jnp.where(turn == 2, -1.0, 0.0))
            sine_neg = jnp.where(turn == 1, -1.0, jnp.where(turn == 3, 1.0, 0.0))
            return cosine * p + sine_neg * q, cosine * q - sine_neg * p

        for t in range(cols // LANES):
            for c, part in enumerate(ghost_tile(at_belt, t)):
                ghost_ref[c, 0:levels, LANES * t : LANES * (t + 1)] = part
        right = lax.rem(at_belt + 1, n_belt)
        before = lax.rem(at_belt + n_belt - 1, n_belt)
        after_tiles = ghost_tile(right, 0)
        before_tiles = ghost_tile(before, cols // LANES - 1)
        lane_row = lax.broadcasted_iota(jnp.int32, (levels, LANES), 1)
        for c in range(2):
            both = jnp.where(lane_row < LANES // 2, after_tiles[c], before_tiles[c])
            ghost_ref[c, 0:levels, cols:] = both

    level = pl.program_id(0)
    at_sub = sub_iota(width)
    winds = []
    for c in range(2):
        pass

    def field_index(c):
        return c * levels + level

    del field_index
    for lev in range(levels):

        @pl.when(level == lev)
        def _(lev=lev):
            winds = []
            for c in range(2):
                index = c * levels + lev
                ghost = ghost_ref[c, lev : lev + 1, :]

                def piece(at, index=index, ghost=ghost):
                    rows_at = band(at, index)
                    if halves == 1 or at == 1:
                        rows_at = jnp.where(first & (at_sub == SUB - 1), ghost, rows_at)
                    if at == 0:
                        rows_at = jnp.where(last & (at_sub == 0), ghost, rows_at)
                    return rows_at

                winds.append(slab(wind_ref[c, lev].astype(F32), index, piece))
            metric = km_ref[2]
            u, v = winds
            across_u = pltpu.roll(u, height - 1, 0) - pltpu.roll(u, 1, 0)
            across_v = pltpu.roll(v, height - 1, 0) - pltpu.roll(v, 1, 0)
            belt_u = pltpu.roll(u, width - 1, 1) - pltpu.roll(u, 1, 1)
            belt_v = pltpu.roll(v, width - 1, 1) - pltpu.roll(v, 1, 1)
            values = [metric * (across_u - belt_v), -metric * (belt_u + across_v)]
            for _ in range(STEPS):
                updated = []
                for c, f in enumerate(values):
                    updated.append(
                        coef_ref[c, 0] * f
                        + coef_ref[c, 1] * pltpu.roll(f, width - 1, 1)
                        + coef_ref[c, 2] * pltpu.roll(f, 1, 1)
                        + coef_ref[c, 3] * pltpu.roll(f, height - 1, 0)
                        + coef_ref[c, 4] * pltpu.roll(f, 1, 0)
                    )
                values = updated
            for c in range(2):
                out_ref[c, 0] = values[c][:rows, :cols]


def per_device(wind, metric, kappa, edge_peer, edge_flip, edge_turn):
    _, levels, rows, cols = wind.shape
    n_across, n_belt = lax.axis_size("across"), lax.axis_size("belt")
    at_across, at_belt = lax.axis_index("across"), lax.axis_index("belt")
    halves = 1 if n_across == 2 else 2
    bands = 2 * levels + 6
    corner_rows = 16 * (-(-bands // (2 * SLOTS)))

    blocks = jnp.arange(n_belt, dtype=jnp.int32)
    if n_belt == 4:
        offset = blocks ^ at_belt
        slot_of = jnp.where(offset == 2, 3, jnp.where(offset == 3, 2, offset))
    else:
        slot_of = blocks
    table = jnp.stack([edge_peer, edge_flip, edge_turn], axis=-1).reshape(-1)
    head = jnp.stack([at_belt, at_across, jnp.int32(n_across), jnp.int32(n_belt)])
    place = jnp.concatenate([head.astype(jnp.int32), table, slot_of.astype(jnp.int32)])

    vmem = pl.BlockSpec(memory_space=pltpu.VMEM)
    smem = pl.BlockSpec(memory_space=pltpu.SMEM)
    bulk, corner, side, rim = pl.pallas_call(
        functools.partial(pack_kernel, "pick" if halves == 1 else "both"),
        out_shape=[
            jax.ShapeDtypeStruct((halves, SUB * bands, cols), BF),
            jax.ShapeDtypeStruct((halves, corner_rows, LANES), BF),
            jax.ShapeDtypeStruct((32, cols), BF),
            jax.ShapeDtypeStruct((16, cols), BF),
        ],
        in_specs=[smem, vmem, vmem, vmem],
        out_specs=[vmem] * 4,
        compiler_params=pltpu.CompilerParams(vmem_limit_bytes=32 << 20),
        name="pack",
    )(place, wind, metric, kappa)

    pairs_a = [(i, i ^ 1) for i in range(n_belt)]
    pairs_b = [(i, ((i ^ 1) + 2 * (i % 2) - 2 * (1 - i % 2)) % n_belt) for i in range(n_belt)]
    pairs_b = [(i, (i + 1) % n_belt if i % 2 else (i - 1) % n_belt) for i in range(n_belt)]
    if halves == 1:
        swap = [(0, 1), (1, 0)]
        corner_in = lax.ppermute(corner, "across", swap)
        bulk_in = lax.ppermute(bulk, "across", swap)
    else:
        onward = [(i, i + 1) for i in range(n_across - 1)]
        back = [(i + 1, i) for i in range(n_across - 1)]

        def both_ways(message):
            return jnp.stack(
                [
                    lax.ppermute(message[1], "across", back),
                    lax.ppermute(message[0], "across", onward),
                ]
            )

        corner_in, bulk_in = both_ways(corner), both_ways(bulk)
    side_a = lax.ppermute(side, "belt", pairs_a)
    side_b = lax.ppermute(side, "belt", pairs_b)
    corner_a = lax.ppermute(corner_in, "belt", pairs_a)
    corner_b = lax.ppermute(corner_in, "belt", pairs_b)
    if n_belt == 4:
        rim_c = lax.ppermute(rim, "belt", [(i, i ^ 2) for i in range(n_belt)])
        rims = jnp.stack([rim, side_a[:16], side_b[:16], rim_c])
    else:
        rims = lax.all_gather(rim, "belt")

    height, width = rows + SUB * halves, cols + LANES
    whole = lambda shape: pl.BlockSpec(shape, lambda i: (0,) * len(shape))
    operands = [wind, metric, kappa, bulk_in, side_a, side_b, corner_a, corner_b, rims]
    return pl.pallas_call(
        functools.partial(main_kernel, halves, n_belt),
        grid=(levels,),
        out_shape=jax.ShapeDtypeStruct((2, levels, rows, cols), F32),
        in_specs=[smem] + [whole(x.shape) for x in operands],
        out_specs=pl.BlockSpec((2, 1, rows, cols), lambda i: (0, i, 0, 0)),
        scratch_shapes=[
            pltpu.VMEM((3, height, width), F32),
            pltpu.VMEM((2, 5, height, width), F32),
            pltpu.VMEM((2, SUB, width), F32),
        ],
        compiler_params=pltpu.CompilerParams(vmem_limit_bytes=48 << 20),
        name="diffuse",
    )(place, *operands)


def solution(mesh):
    return jax.shard_map(
        per_device,
        mesh=mesh,
        in_specs=(
            P(None, ("members", "lev"), "across", "belt"),
            P("across", "belt"),
            P(None, "across", "belt"),
            P(),
            P(),
            P(),
        ),
        out_specs=P(None, ("members", "lev"), "across", "belt"),
        check_vma=False,
    )
```

```python
import functools

import jax
import jax.numpy as jnp
import numpy as np
from jax import lax
from jax.experimental import pallas as pl
from jax.experimental.pallas import tpu as pltpu
from jax.sharding import PartitionSpec as P

STEPS = 6
LANES = 128
SUB = 8
SLOTS = 8
BF = jnp.bfloat16
F32 = jnp.float32
MARGIN = STEPS + 1
WINDOW = 3 * LANES
PACK_LIMIT = 8 << 20
MID_LIMIT = 20 << 20
EDGE_LIMIT = 20 << 20
MIDDLE_FROM, MIDDLE_TO = 4 * LANES - (WINDOW - 2 * MARGIN), 4 * LANES + (WINDOW - 2 * MARGIN)
MIDDLES = [(1, MIDDLE_FROM - MARGIN - LANES, 0), (3, LANES - MARGIN, 1)]


def split_hi_lo(value):
    hi = value.astype(BF).astype(F32)
    return hi, value - hi


def lane_iota():
    return lax.broadcasted_iota(jnp.int32, (SUB, LANES), 1)


def sub_iota(width):
    return lax.broadcasted_iota(jnp.int32, (SUB, width), 0)


def compact(tiles):
    slot = lane_iota() // 16
    packed = []
    for at in range(0, len(tiles), SLOTS):
        total = None
        for g, tile in enumerate(tiles[at : at + SLOTS]):
            moved = pltpu.roll(tile, (8 + 16 * g) % LANES, 1)
            total = moved if total is None else jnp.where(slot == g, moved, total)
        packed.append(total)
    return packed


def fetched(pairs, sems):
    copies = [pltpu.make_async_copy(src, dst, sems.at[i]) for i, (src, dst) in enumerate(pairs)]
    for copy in copies:
        copy.start()
    return copies


def edge_tile(band):
    left = lax.broadcasted_iota(jnp.int32, (band.shape[0], LANES), 1) < LANES // 2
    return jnp.where(left, band[:, :LANES], band[:, band.shape[1] - LANES :])


def compact_rows(tiles):
    packed = compact(tiles)
    packed += [jnp.zeros((SUB, LANES), F32)] * (-len(packed) % 2)
    return [jnp.concatenate(packed[i : i + 2], axis=0).astype(BF) for i in range(0, len(packed), 2)]


def pack_kernel(
    halves, ends_col, wind_hbm, metric_hbm, kappa_hbm, peer_hbm,
    bulk_ref, corner_ref, rim_ref, side_ref, own_ref, pick_ref, *scratch
):
    wind_ref, kappa_ref, metric_ref, peer_ref, sems = scratch
    levels, rows, cols = wind_hbm.shape[1:]
    first = lax.axis_index("across") == 0
    pairs = [(wind_hbm, wind_ref), (kappa_hbm, kappa_ref), (metric_hbm, metric_ref), (peer_hbm, peer_ref)]
    for copy in fetched(pairs, sems):
        copy.wait()
    at_belt = lax.axis_index("belt")
    wanted = peer_ref[jnp.where(first, 0, 1), at_belt ^ 1]
    pick_ref[...] = jnp.full(pick_ref.shape, jnp.where(wanted == at_belt, 1.0, 0.0), BF)
    top, bottom = slice(0, SUB), slice(rows - SUB, rows)

    def bands_of(whole):
        if halves == 1:
            return [jnp.where(first, whole[bottom], whole[top])]
        return [whole[bottom], whole[top]]

    pieces, tiles, rim_rows = [[] for _ in range(halves)], [], []
    for f in range(2 * levels):
        own_ref[rows * f : rows * (f + 1)] = wind_ref[f // levels, f % levels]
        whole = wind_ref[f // levels, f % levels].astype(F32)
        for k, band in enumerate(bands_of(whole)):
            pieces[k].append(band)
        tiles += [edge_tile(whole[r : r + SUB]) for r in range(0, rows, SUB)]
        rim_rows.append(jnp.where(first, whole[0:1], whole[rows - 1 : rows]))
    for q in range(3):
        for half, part in enumerate(split_hi_lo(kappa_ref[q] if q < 2 else metric_ref[...])):
            at = rows * (2 * levels + 2 * q + half)
            own_ref[at : at + rows] = part.astype(BF)
            for k, band in enumerate(bands_of(part)):
                pieces[k].append(band)
            tiles += [edge_tile(part[r : r + SUB]) for r in range(0, rows, SUB)]
    for k in range(halves):
        for i in range(0, len(pieces[k]), 2):
            both = jnp.concatenate([pieces[k][i], pieces[k][i + 1]], axis=0)
            bulk_ref[k, SUB * i : SUB * (i + 2)] = both.astype(BF)
        for i, tile in enumerate(compact_rows([edge_tile(p) for p in pieces[k]])):
            corner_ref[k, :, LANES * i : LANES * (i + 1)] = tile
    rim = jnp.concatenate(rim_rows + [jnp.zeros((16 - len(rim_rows), cols), F32)], axis=0)
    rim_ref[...] = rim.astype(BF)
    side_ref[...] = jnp.zeros(side_ref.shape, BF)
    for i, tile in enumerate(compact_rows(tiles)):
        side_ref[:, LANES * i : LANES * (i + 1)] = tile
    if ends_col is not None:
        side_ref[:, ends_col : ends_col + LANES] = edge_tile(rim).astype(BF)


def rim_slot(block, at_belt, n_belt):
    if n_belt != 4:
        return block
    return jnp.where(block == at_belt, 0, jnp.where((block ^ at_belt) == 2, 2, 1))


def end_slot(block, at_belt, n_belt):
    if n_belt != 4:
        return block
    offset = block ^ at_belt
    return jnp.where(offset == 2, 3, jnp.where(offset == 3, 2, offset))


class Rows:
    def __init__(self, levels, rows, halves):
        self.levels, self.rows, self.halves = levels, rows, halves
        self.fields, self.bands = 2 * levels, 2 * levels + 6
        self.tiles, self.span = rows // SUB, SUB * halves
        self.slab = self.tiles + halves
        self.height = SUB * self.slab

    def own_base(self, f):
        return 2 * self.height * (f // 2) + (self.height + self.span) * (f % 2)

    def band_base(self, f):
        return 2 * self.height * (f // 2) + self.rows

    def place_of(self, f, e):
        return e if f % 2 == 0 else (e + self.halves) % self.slab


def east_of(f):
    return [f[1], f[2], pltpu.roll(f[0], LANES - 1, 1)]


def west_of(f):
    return [pltpu.roll(f[2], 1, 1), f[0], f[1]]


def fill_order(order_ref, source_of):
    size = order_ref.shape[0]
    at = lax.broadcasted_iota(jnp.int32, (size, LANES), 0)
    lane = lax.broadcasted_iota(jnp.int32, (1, LANES), 1)
    for r in range(3):
        tile = jnp.where(at == source_of(3 * lane + r), 1.0, 0.0).astype(BF)
        order_ref[:, LANES * r : LANES * (r + 1)] = tile
        order_ref[:, LANES * (3 + r) : LANES * (4 + r)] = tile


def solve_window(lay, first, last, x_ref, order_ref, work):
    y_ref, coef_ref, met_ref, even_ref, odd_ref, fin_ref, z_ref = work
    levels, rows, fields, tiles = lay.levels, lay.rows, lay.fields, lay.tiles
    slab, height, span = lay.slab, lay.height, lay.span
    sub = lax.broadcasted_iota(jnp.int32, (SUB, LANES), 0)
    sub_slab = lax.broadcasted_iota(jnp.int32, (height, LANES), 0)
    closed = ((sub_slab == rows - 1) & last) | ((sub_slab == height - 1) & first)

    def put(ref, f, r, i, value):
        ref[f, r, SUB * (i + 1) : SUB * (i + 2)] = value
        if i == 0:
            ref[f, r, SUB * (slab + 1) : SUB * (slab + 2)] = value
        if i == slab - 1:
            ref[f, r, 0:SUB] = value
        if r == 0:
            return [(ref, f, 3, i, pltpu.roll(value, LANES - 1, 1))]
        if r == 2:
            return [(ref, f, 4, i, pltpu.roll(value, 1, 1))]
        return []

    def flush(rotated):
        for ref, f, plane, i, value in rotated:
            ref[f, plane, SUB * (i + 1) : SUB * (i + 2)] = value

    def advance(source, target, final):
        waiting = []
        for c in range(2):
            for e in range(tiles if final else slab):
                mid, east, west, south, north = (
                    [coef_ref[c, k, r, SUB * e : SUB * (e + 1)] for r in range(3)] for k in range(5)
                )
                results = []
                for lev in range(levels):
                    f = c * levels + lev
                    at = SUB * (lay.place_of(f, e) + 1)
                    here = [source[f, r, at : at + SUB] for r in range(5)]
                    right, left = [here[1], here[2], here[3]], [here[4], here[0], here[1]]
                    results.append(
                        [
                            (mid[r] * here[r] + south[r] * source[f, r, at + 1 : at + 1 + SUB])
                            + north[r] * source[f, r, at - 1 : at - 1 + SUB]
                            + (east[r] * right[r] + west[r] * left[r])
                            for r in range(3)
                        ]
                    )
                rotated = []
                for lev in range(levels):
                    f = c * levels + lev
                    for r in range(3):
                        if final:
                            fin_ref[rows * f + SUB * e : rows * f + SUB * (e + 1), LANES * r : LANES * (r + 1)] = results[lev][r]
                        else:
                            rotated += put(target, f, r, lay.place_of(f, e), results[lev][r])
                flush(waiting)
                waiting = rotated
        flush(waiting)

    whole = jnp.dot(x_ref[...], order_ref[:, 0:WINDOW], preferred_element_type=F32)
    for r in range(3):
        y_ref[r] = whole[:, LANES * r : LANES * (r + 1)]
    for q in range(3):
        base = height * (fields + 2 * q)
        low = base + height
        value = [
            y_ref[r, base : base + height]
            + jnp.concatenate([y_ref[r, low + span : low + height], y_ref[r, low : low + span]], axis=0)
            for r in range(3)
        ]
        if q == 2:
            for r in range(3):
                met_ref[r] = 0.5 * value[r]
            continue
        right = east_of(value)
        east = [0.5 * (value[r] + right[r]) for r in range(3)]
        west = west_of(east)
        for r in range(3):
            south = jnp.where(closed, 0.0, 0.5 * (value[r] + pltpu.roll(value[r], height - 1, 0)))
            north = pltpu.roll(south, 1, 0)
            coef_ref[q, 0, r] = 1.0 - ((east[r] + west[r]) + (south + north))
            coef_ref[q, 1, r] = east[r]
            coef_ref[q, 2, r] = west[r]
            coef_ref[q, 3, r] = south
            coef_ref[q, 4, r] = north
    waiting = []
    for e in range(slab):
        rotated = []
        metric = [met_ref[r, SUB * e : SUB * (e + 1)] for r in range(3)]
        for lev in range(levels):
            across, belt = [], []
            for c in range(2):
                f = c * levels + lev
                base, i = height * f, lay.place_of(f, e)
                at = base + SUB * i
                here = [y_ref[r, at : at + SUB] for r in range(3)]
                right, left = east_of(here), west_of(here)
                belt.append([right[r] - left[r] for r in range(3)])
                diffs = []
                for r in range(3):
                    if i < slab - 1:
                        below = y_ref[r, at + 1 : at + 1 + SUB]
                    else:
                        wrap = pltpu.roll(y_ref[r, base : base + SUB], SUB - 1, 0)
                        below = jnp.where(sub == SUB - 1, wrap, pltpu.roll(here[r], SUB - 1, 0))
                    if i > 0:
                        above = y_ref[r, at - 1 : at - 1 + SUB]
                    else:
                        end = base + height
                        wrap = pltpu.roll(y_ref[r, end - SUB : end], 1, 0)
                        above = jnp.where(sub == 0, wrap, pltpu.roll(here[r], 1, 0))
                    diffs.append(below - above)
                across.append(diffs)
            for r in range(3):
                curl = metric[r] * (across[0][r] - belt[1][r])
                divergence = metric[r] * (-belt[0][r] - across[1][r])
                rotated += put(even_ref, lev, r, lay.place_of(lev, e), curl)
                rotated += put(even_ref, levels + lev, r, lay.place_of(levels + lev, e), divergence)
        flush(waiting)
        waiting = rotated
    flush(waiting)

    def two(k, _):
        advance(even_ref, odd_ref, False)
        advance(odd_ref, even_ref, False)
        return 0

    lax.fori_loop(0, STEPS // 2 - 1, two, 0)
    advance(even_ref, odd_ref, False)
    advance(odd_ref, None, True)
    value = fin_ref[...]
    hi = value.astype(BF)
    z_ref[:, 0 : 3 * LANES] = hi
    z_ref[:, 3 * LANES :] = (value - hi.astype(F32)).astype(BF)


def work_shapes(lay):
    return [
        pltpu.VMEM((3, lay.height * lay.bands, LANES), F32),
        pltpu.VMEM((2, 5, 3, lay.height, LANES), F32),
        pltpu.VMEM((3, lay.height, LANES), F32),
        pltpu.VMEM((lay.fields, 5, lay.height + 2 * SUB, LANES), F32),
        pltpu.VMEM((lay.fields, 5, lay.height + 2 * SUB, LANES), F32),
        pltpu.VMEM((lay.rows * lay.fields, WINDOW), F32),
        pltpu.VMEM((lay.rows * lay.fields, 2 * WINDOW), BF),
    ]


def back_to_natural(z, order, cols):
    return lax.dot_general(z, order[cols], (((1,), (1,)), ((), ())), preferred_element_type=F32)


def ghost_tile_at(lay, first):
    return pl.multiple_of(jnp.where(first, 0, lay.rows - SUB), SUB)


def middle_kernel(
    lay, tile, offset, keep, own_ref, bulk_ref, after_ref,
    out_ref, order_ref, coef_out, met_out, x_ref, *work,
):
    del after_ref
    first, last = lax.axis_index("across") == 0, lax.axis_index("across") == lax.axis_size("across") - 1
    cols = slice(LANES * tile, LANES * (tile + 4))
    fill_order(order_ref, lambda place: place + offset)
    for f in range(lay.bands):
        base = lay.own_base(f)
        x_ref[base : base + lay.rows] = own_ref[lay.rows * f : lay.rows * (f + 1), cols]
    span = lay.span
    at_row = lax.broadcasted_iota(jnp.int32, (2 * span, 4 * LANES), 0)
    for f in range(0, lay.bands, 2):
        band = bulk_ref[span * f : span * (f + 2), cols]
        if f < lay.fields:
            band = band.astype(F32)
            for k in range(2):
                spot = jnp.where(first, span * (k + 1) - 1, jnp.where(last, span * k, -1))
                band = jnp.where(at_row == spot, 0.0, band)
            band = band.astype(BF)
        at = lay.band_base(f)
        x_ref[at : at + 2 * span] = band
    solve_window(lay, first, last, x_ref, order_ref, work)
    back = back_to_natural(work[-1][...], order_ref, slice(LANES * keep, LANES * (keep + 3)))
    for f in range(lay.fields):
        out_ref[f // lay.levels, f % lay.levels] = back[lay.rows * f : lay.rows * (f + 1)]
    at = ghost_tile_at(lay, first)
    coef_out[...] = work[1][:, :, :, pl.ds(at, SUB)]
    met_out[...] = work[2][:, pl.ds(at, SUB)]


def edge_kernel(lay, n_belt, relay, plan, peer_ref, flip_ref, turn_ref, own_ref, bulk_ref, *rest):
    if relay is None:
        side_a_ref, side_b_ref, corner_a_ref, corner_b_ref, rims_ref, ends_ref, *rest = rest
    else:
        rim_ref, side_ref, far_ref, near_ref, *rest = rest
        *rest, rims_ref, ends_ref = rest
        corner_at, ends_at = relay
        side_a_ref, side_b_ref = near_ref.at[16:32], near_ref.at[32:48]
        corner_a_ref, corner_b_ref = (
            near_ref.at[pl.ds(k, 16), corner_at:ends_at] for k in (16, 32)
        )
        for k, rim in enumerate((rim_ref[...], near_ref[0:16], far_ref[0:16])):
            rims_ref[k] = rim
        ends_cols = slice(ends_at, ends_at + LANES)
        for k, (ref, at) in enumerate(((side_ref, 0), (near_ref, 16), (near_ref, 32), (far_ref, 16))):
            ends_ref[k] = ref[at : at + 16, ends_cols]
    middles, rest = [rest[4 * k : 4 * k + 4] for k in range(2)], rest[8:]
    out_hbm, x_ref, order_ref, ghost_ref, grow_ref, ext_ref, strip_ref, sems, *work = rest
    levels, rows, cols = lay.levels, lay.rows, own_ref.shape[1]
    tiles, halves, fields, bands, span = lay.tiles, lay.halves, lay.fields, lay.bands, lay.span
    at_belt, at_across = lax.axis_index("belt"), lax.axis_index("across")
    first, last = at_across == 0, at_across == lax.axis_size("across") - 1
    ghost_at = ghost_tile_at(lay, first)
    rest_at = pl.multiple_of(jnp.where(first, SUB, 0), SUB)
    calm = pl.ds(rest_at, rows - SUB)
    left_end, split, right_start, right_end = plan
    early = [
        pltpu.make_async_copy(
            middles[0][0].at[:, :, calm, LANES:], out_hbm.at[:, :, calm, left_end:split], sems.at[0]
        ),
        pltpu.make_async_copy(
            middles[1][0].at[:, :, calm, : 2 * LANES], out_hbm.at[:, :, calm, split:right_start], sems.at[1]
        ),
    ]
    for copy in early:
        copy.start()
    even = lax.rem(at_belt, 2) == 0
    from_right = (lane_iota() // 8) % 2 == 1
    take_a = from_right == even

    def unpacked(a_ref, b_ref, groups):
        out = []
        for g in range(groups):
            column, half = LANES * (g // 2), slice(SUB * (g % 2), SUB * (g % 2) + SUB)
            a = a_ref(column).astype(F32)[half]
            b = b_ref(column).astype(F32)[half]
            out.append(jnp.where(take_a, a, b))
        return out

    def put_back(packed, index):
        return pltpu.roll(packed[index // SLOTS], (-(8 + 16 * (index % SLOTS))) % LANES, 1)

    ghost_ref[...] = jnp.zeros(ghost_ref.shape, F32)
    edge = jnp.where(first, 0, 1)
    lane_r = lax.broadcasted_iota(jnp.int32, (LANES, LANES), 0)
    lane_c = lax.broadcasted_iota(jnp.int32, (LANES, LANES), 1)
    backward = jnp.where(lane_r + lane_c == LANES - 1, 1.0, 0.0).astype(BF)
    blocks = [at_belt, lax.rem(at_belt + 1, n_belt), lax.rem(at_belt + n_belt - 1, n_belt)]
    peers = [peer_ref[edge, block] for block in blocks]
    own_rim = rims_ref[rim_slot(peers[0], at_belt, n_belt)]
    col_tiles = cols // LANES
    raw = [own_rim[:, LANES * t : LANES * (t + 1)] for t in range(col_tiles)]
    raw += [ends_ref[end_slot(peer, at_belt, n_belt)] for peer in peers[1:]]
    turned = jnp.dot(jnp.concatenate(raw, axis=0), backward, preferred_element_type=F32)

    def ghost_parts(block, plain, flipped):
        flip, turn = flip_ref[edge, block], turn_ref[edge, block]
        found = jnp.where(flip == 1, turned[16 * flipped : 16 * (flipped + 1)], raw[plain].astype(F32))
        p, q = found[0:levels], found[levels : 2 * levels]
        cosine = jnp.where(turn == 0, 1.0, jnp.where(turn == 2, -1.0, 0.0))
        sine_neg = jnp.where(turn == 1, -1.0, jnp.where(turn == 3, 1.0, 0.0))
        return cosine * p + sine_neg * q, cosine * q - sine_neg * p

    for t in range(col_tiles):
        for c, part in enumerate(ghost_parts(blocks[0], t, col_tiles - 1 - t)):
            ghost_ref[c, 0:levels, LANES * t : LANES * (t + 1)] = part
    after_tiles = ghost_parts(blocks[1], col_tiles, col_tiles)
    before_tiles = ghost_parts(blocks[2], col_tiles + 1, col_tiles + 1)
    lane_row = lax.broadcasted_iota(jnp.int32, (levels, LANES), 1)
    for c in range(2):
        both = jnp.where(lane_row < LANES // 2, after_tiles[c], before_tiles[c])
        ghost_ref[c, 0:levels, cols:] = both

    side_tiles = unpacked(
        lambda k: side_a_ref[:, k : k + LANES], lambda k: side_b_ref[:, k : k + LANES],
        -(-bands * tiles // SLOTS),
    )
    corners = [
        unpacked(
            lambda k, at=at: (corner_a_ref if relay else corner_a_ref.at[at])[:, k : k + LANES],
            lambda k, at=at: (corner_b_ref if relay else corner_b_ref.at[at])[:, k : k + LANES],
            -(-bands // SLOTS),
        )
        for at in range(halves)
    ]
    near_start, near_end = slice(0, 2 * LANES), slice(cols - 2 * LANES, cols)
    for part, place in ((near_start, slice(LANES, 3 * LANES)), (near_end, slice(3 * LANES, 5 * LANES))):
        for f in range(bands):
            base = lay.own_base(f)
            x_ref[base : base + rows, place] = own_ref[rows * f : rows * (f + 1), part]
    for f in range(bands):
        halo = jnp.concatenate([put_back(side_tiles, f * tiles + r) for r in range(tiles)], axis=0)
        x_ref[lay.own_base(f) : lay.own_base(f) + rows, 0:LANES] = halo.astype(BF)
    at_row = lax.broadcasted_iota(jnp.int32, (2 * span, 5 * LANES), 0)
    for f in range(0, bands, 2):
        body = bulk_ref[span * f : span * (f + 2)].astype(F32)
        halo = jnp.concatenate(
            [put_back(corners[at], f + k) for k in range(2) for at in range(halves)], axis=0
        )
        band = jnp.concatenate([halo, body[:, near_start], body[:, near_end]], axis=1)
        if f < fields:
            for k in range(2):
                c, lev = (f + k) // levels, (f + k) % levels
                row = ghost_ref[c, lev : lev + 1, :]
                row = jnp.concatenate([row[:, cols:], row[:, near_start], row[:, near_end]], axis=1)
                spot = jnp.where(first, span * (k + 1) - 1, jnp.where(last, span * k, -1))
                band = jnp.where(at_row == spot, row, band)
        x_ref[lay.band_base(f) : lay.band_base(f) + 2 * span] = band.astype(BF)

    half, size = WINDOW // 2, 5 * LANES

    def source_of(place):
        at_left = place + LANES - MARGIN
        at_right = place + size - (WINDOW - MARGIN)
        return jnp.where(place < half, at_left, jnp.where(at_right < size, at_right, at_right - size))

    fill_order(order_ref, source_of)

    sub = lax.broadcasted_iota(jnp.int32, (SUB, LANES), 0)
    spot = jnp.where(first, 0, SUB - 1)
    sign = jnp.where(first, -1.0, jnp.where(last, 1.0, 0.0))
    lift = jnp.where(sub == spot, sign, 0.0)
    values = []
    for k, (_, order, coef, met) in enumerate(middles):
        cols_k = slice(LANES * MIDDLES[k][0], LANES * (MIDDLES[k][0] + 4))
        rows_k = jnp.concatenate([ghost_ref[0, :, cols_k], ghost_ref[1, :, cols_k]], axis=0).astype(BF)
        found = jnp.dot(rows_k, order[:, 0:WINDOW], preferred_element_type=F32)
        for f in range(fields):
            c, lev = f // levels, f % levels
            row = found[SUB * c + lev : SUB * c + lev + 1]
            scale = [(1.0 - 2.0 * c) * lift * met[r] for r in range(3)]
            values.append([scale[r] * row[:, LANES * r : LANES * (r + 1)] for r in range(3)])
    inner_south, inner_north = sub < SUB - 1, sub > 0
    for _ in range(STEPS):
        updated = []
        for at, f in enumerate(values):
            coef, c = middles[at // fields][2], at % fields // levels
            right, left = east_of(f), west_of(f)
            updated.append(
                [
                    (coef[c, 0, r] * f[r] + coef[c, 1, r] * right[r] + coef[c, 2, r] * left[r])
                    + jnp.where(inner_south, coef[c, 3, r], 0.0) * pltpu.roll(f[r], SUB - 1, 0)
                    + jnp.where(inner_north, coef[c, 4, r], 0.0) * pltpu.roll(f[r], 1, 0)
                    for r in range(3)
                ]
            )
        values = updated
    for at, f in enumerate(values):
        for r in range(3):
            grow_ref[SUB * at : SUB * (at + 1), LANES * r : LANES * (r + 1)] = f[r]
    strips = []
    for k in range(2):
        grown = grow_ref[SUB * fields * k : SUB * fields * (k + 1)]
        hi = grown.astype(BF)
        parts = jnp.concatenate([hi, (grown - hi.astype(F32)).astype(BF)], axis=1)
        keep = MIDDLES[k][2]
        strips.append(back_to_natural(parts, middles[k][1], slice(LANES * keep, LANES * (keep + 3))))
    for f in range(fields):
        c, lev = f // levels, f % levels
        for k, part in ((0, slice(LANES, WINDOW)), (1, slice(0, 2 * LANES))):
            added = strips[k][SUB * f : SUB * (f + 1), part]
            strip_ref[c, lev, :, 2 * LANES * k : 2 * LANES * (k + 1)] = (
                middles[k][0][c, lev, pl.ds(ghost_at, SUB), part] + added
            )
    edge_rows = pl.ds(ghost_at, SUB)
    strip_copy = pltpu.make_async_copy(
        strip_ref, out_hbm.at[:, :, edge_rows, left_end:right_start], sems.at[2]
    )
    strip_copy.start()

    solve_window(lay, first, last, x_ref, order_ref, work)
    back = back_to_natural(work[-1][...], order_ref, slice(LANES, 5 * LANES))
    lane = lax.broadcasted_iota(jnp.int32, (rows, LANES), 1)
    lane_tile = lane[:SUB]
    low, high = MIDDLE_FROM - LANES, right_end - right_start
    for f in range(fields):
        c, lev = f // levels, f % levels
        mine = back[rows * f : rows * (f + 1)]
        ext_ref[c, lev, :, 0:LANES] = mine[:, 0:LANES]
        ext_ref[c, lev, :, 3 * LANES :] = mine[:, 3 * LANES :]
        one, two = slice(LANES, 2 * LANES), slice(2 * LANES, 3 * LANES)
        ext_ref[c, lev, :, one] = jnp.where(lane < low, mine[:, one], middles[0][0][c, lev, :, 0:LANES])
        ext_ref[c, lev, :, two] = jnp.where(lane >= high, mine[:, two], middles[1][0][c, lev, :, 2 * LANES :])
        for k, (place, mask, part) in enumerate(
            ((one, lane_tile >= low, slice(0, LANES)), (two, lane_tile < high, slice(2 * LANES, WINDOW)))
        ):
            added = strips[k][SUB * f : SUB * (f + 1), part]
            ext_ref[c, lev, edge_rows, place] = ext_ref[c, lev, edge_rows, place] + jnp.where(mask, added, 0.0)
    late = [
        pltpu.make_async_copy(ext_ref.at[:, :, :, : 2 * LANES], out_hbm.at[:, :, :, :left_end], sems.at[3]),
        pltpu.make_async_copy(ext_ref.at[:, :, :, 2 * LANES :], out_hbm.at[:, :, :, right_start:], sems.at[4]),
    ]
    for copy in late:
        copy.start()
    for copy in early + [strip_copy] + late:
        copy.wait()


def per_device(wind, metric, kappa, edge_peer, edge_flip, edge_turn):
    _, levels, rows, cols = wind.shape
    n_across, n_belt = lax.axis_size("across"), lax.axis_size("belt")
    halves = 1 if n_across == 2 else 2
    fields = 2 * levels
    bands = fields + 6
    corner_cols = LANES * (-(-bands // (2 * SLOTS)))
    side_cols = LANES * (-(-bands * (rows // SUB) // (2 * SLOTS)))
    ends_col = side_cols + corner_cols
    relay = halves == 1 and n_belt == 4 and ends_col + LANES <= cols

    vmem = pl.BlockSpec(memory_space=pltpu.VMEM)
    smem = pl.BlockSpec(memory_space=pltpu.SMEM)
    anywhere = pl.BlockSpec(memory_space=pl.ANY)
    lay = Rows(levels, rows, halves)
    height, span = lay.height, lay.span
    bulk, corner, rim, side, own, pick = pl.pallas_call(
        functools.partial(pack_kernel, halves, ends_col if relay else None),
        out_shape=[
            jax.ShapeDtypeStruct((halves, SUB * bands, cols), BF),
            jax.ShapeDtypeStruct((halves, 16, corner_cols), BF),
            jax.ShapeDtypeStruct((16, cols), BF),
            jax.ShapeDtypeStruct((16, cols), BF),
            jax.ShapeDtypeStruct((rows * bands, cols), BF),
            jax.ShapeDtypeStruct((16, cols), BF),
        ],
        in_specs=[anywhere] * 4,
        out_specs=[vmem] * 6,
        scratch_shapes=[
            pltpu.VMEM(wind.shape, BF),
            pltpu.VMEM(kappa.shape, F32),
            pltpu.VMEM(metric.shape, F32),
            pltpu.SMEM(edge_peer.shape, jnp.int32),
            pltpu.SemaphoreType.DMA((4,)),
        ],
        compiler_params=pltpu.CompilerParams(vmem_limit_bytes=PACK_LIMIT),
        name="pack",
    )(*(pltpu.with_memory_space_constraint(x, pltpu.HBM) for x in (wind, metric, kappa, edge_peer)))

    pairs_a = [(i, i ^ 1) for i in range(n_belt)]
    pairs_b = [(i, (i + 1) % n_belt if i % 2 else (i - 1) % n_belt) for i in range(n_belt)]
    if halves == 1:
        swap = [(0, 1), (1, 0)]
        bulk_in = lax.ppermute(bulk, "across", swap)
        corner_in = lax.ppermute(corner, "across", swap)
    else:
        onward = [(i, i + 1) for i in range(n_across - 1)]
        back = [(i + 1, i) for i in range(n_across - 1)]

        def both_ways(message):
            return jnp.stack(
                [
                    lax.ppermute(message[1], "across", back),
                    lax.ppermute(message[0], "across", onward),
                ]
            )

        corner_in, bulk_in = both_ways(corner), both_ways(bulk)
    bulk_in = bulk_in.reshape(halves, bands, SUB, cols).swapaxes(0, 1).reshape(bands * span, cols)

    def middle(k, after):
        tile, offset, keep = MIDDLES[k]
        shapes = [
            jax.ShapeDtypeStruct((2, levels, rows, WINDOW), F32),
            jax.ShapeDtypeStruct((4 * LANES, 2 * WINDOW), BF),
            jax.ShapeDtypeStruct((2, 5, 3, SUB, LANES), F32),
            jax.ShapeDtypeStruct((3, SUB, LANES), F32),
        ]
        return pl.pallas_call(
            functools.partial(middle_kernel, lay, tile, offset, keep),
            out_shape=shapes,
            in_specs=[vmem] * 2 + [anywhere],
            out_specs=[vmem] * len(shapes),
            scratch_shapes=[pltpu.VMEM((height * bands, 4 * LANES), BF)] + work_shapes(lay),
            compiler_params=pltpu.CompilerParams(vmem_limit_bytes=MID_LIMIT),
            cost_estimate=pl.CostEstimate(flops=2_000_000_000, bytes_accessed=2_000_000, transcendentals=0),
            name="middle",
        )(own, bulk_in, after)

    if relay:
        spot = slice(side_cols, ends_col)
        side = jnp.concatenate([side[:, :side_cols], corner_in[0], side[:, ends_col:]], axis=1)
        far = lax.ppermute(jnp.concatenate([rim, side]), "belt", [(i, i ^ 2) for i in range(n_belt)])
        rim_c, side_c = far[:16], far[16:]
        chosen = jnp.where(pick > 0, rim, rim_c)
        near = lax.ppermute(jnp.concatenate([chosen, side, side_c]), "belt", pairs_a)
        middle_0 = middle(0, corner_in)
        middle_1 = middle(1, corner_in)
        messages = [rim, side, far, near]
    else:
        side_a = lax.ppermute(side, "belt", pairs_a)
        side_b = lax.ppermute(side, "belt", pairs_b)
        corner_a = lax.ppermute(corner_in, "belt", pairs_a)
        corner_b = lax.ppermute(corner_in, "belt", pairs_b)
        rims = lax.all_gather(rim, "belt")
        if n_belt == 4:
            at_belt = lax.axis_index("belt")
            rims, ends = (rims[at_belt ^ jnp.array([0, 1, 2])], rims[at_belt ^ jnp.array([0, 1, 3, 2])])
        else:
            ends = rims
        ends = jnp.concatenate([ends[..., : LANES // 2], ends[..., cols - LANES // 2 :]], axis=-1)

        messages = [side_a, side_b, corner_a, corner_b, rims, ends]
        middle_0, middle_1 = middle(0, corner_in), middle(1, corner_in)
    operands = [own, bulk_in, *messages, *middle_0, *middle_1]
    own_rims = [pltpu.VMEM((3, 16, cols), BF), pltpu.VMEM((4, 16, LANES), BF)] if relay else []
    plan = (2 * LANES, cols // 2, cols - 2 * LANES, MIDDLE_TO)
    return pl.pallas_call(
        functools.partial(edge_kernel, lay, n_belt, (side_cols, ends_col) if relay else None, plan),
        out_shape=jax.ShapeDtypeStruct((2, levels, rows, cols), F32),
        in_specs=[smem] * 3 + [vmem] * len(operands),
        out_specs=anywhere,
        scratch_shapes=[
            pltpu.VMEM((height * bands, 5 * LANES), BF),
            pltpu.VMEM((5 * LANES, 2 * WINDOW), BF),
            pltpu.VMEM((2, SUB, cols + LANES), F32),
            pltpu.VMEM((2 * fields * SUB, WINDOW), F32),
            pltpu.VMEM((2, levels, rows, 4 * LANES), F32),
            pltpu.VMEM((2, levels, SUB, 4 * LANES), F32),
            pltpu.SemaphoreType.DMA((5,)),
        ]
        + work_shapes(lay)
        + own_rims,
        compiler_params=pltpu.CompilerParams(vmem_limit_bytes=EDGE_LIMIT),
        name="edges",
    )(edge_peer, edge_flip, edge_turn, *operands)


def solution(mesh):
    return jax.shard_map(
        per_device,
        mesh=mesh,
        in_specs=(
            P(None, ("members", "lev"), "across", "belt"),
            P("across", "belt"),
            P(None, "across", "belt"),
            P(),
            P(),
            P(),
        ),
        out_specs=P(None, ("members", "lev"), "across", "belt"),
        check_vma=False,
    )
```

```python
import functools

import jax
import jax.numpy as jnp
import numpy as np
from jax import lax
from jax.experimental import pallas as pl
from jax.experimental.pallas import tpu as pltpu
from jax.sharding import PartitionSpec as P

STEPS = 6
LANES = 128
SUB = 8
SLOTS = 8
BF = jnp.bfloat16
F32 = jnp.float32
MARGIN = STEPS + 1
WINDOW = 3 * LANES
PACK_LIMIT = 8 << 20
MID_LIMIT = 20 << 20
EDGE_LIMIT = 20 << 20
MIDDLE_FROM, MIDDLE_TO = 4 * LANES - (WINDOW - 2 * MARGIN), 4 * LANES + (WINDOW - 2 * MARGIN)
MIDDLES = [(1, MIDDLE_FROM - MARGIN - LANES, 0), (3, LANES - MARGIN, 1)]


def split_hi_lo(value):
    hi = value.astype(BF).astype(F32)
    return hi, value - hi


def lane_iota():
    return lax.broadcasted_iota(jnp.int32, (SUB, LANES), 1)


def sub_iota(width):
    return lax.broadcasted_iota(jnp.int32, (SUB, width), 0)


def compact(tiles):
    slot = lane_iota() // 16
    packed = []
    for at in range(0, len(tiles), SLOTS):
        total = None
        for g, tile in enumerate(tiles[at : at + SLOTS]):
            moved = pltpu.roll(tile, (8 + 16 * g) % LANES, 1)
            total = moved if total is None else jnp.where(slot == g, moved, total)
        packed.append(total)
    return packed


def fetched(pairs, sems):
    copies = [pltpu.make_async_copy(src, dst, sems.at[i]) for i, (src, dst) in enumerate(pairs)]
    for copy in copies:
        copy.start()
    return copies


def edge_tile(band):
    left = lax.broadcasted_iota(jnp.int32, (band.shape[0], LANES), 1) < LANES // 2
    return jnp.where(left, band[:, :LANES], band[:, band.shape[1] - LANES :])


def compact_rows(tiles):
    packed = compact(tiles)
    packed += [jnp.zeros((SUB, LANES), F32)] * (-len(packed) % 2)
    return [jnp.concatenate(packed[i : i + 2], axis=0).astype(BF) for i in range(0, len(packed), 2)]


def bulk_place(t):
    if 1 <= t <= 4:
        return 0, LANES * (t - 1)
    return 1, 0 if t == 0 else LANES * (t - 4)


def bulk_tiles(refs, at, count, tiles):
    parts = []
    for t in tiles:
        part, col = bulk_place(t)
        parts.append(refs[part][at : at + count, col : col + LANES])
    return jnp.concatenate(parts, axis=1)


def pack_kernel(
    halves, ends_col, wind_hbm, metric_hbm, kappa_hbm, peer_hbm,
    bulk_0_ref, bulk_1_ref, corner_ref, rim_ref, side_ref, own_ref, pick_ref, *scratch
):
    wind_ref, kappa_ref, metric_ref, peer_ref, sems = scratch
    levels, rows, cols = wind_hbm.shape[1:]
    first = lax.axis_index("across") == 0
    pairs = [(wind_hbm, wind_ref), (kappa_hbm, kappa_ref), (metric_hbm, metric_ref), (peer_hbm, peer_ref)]
    for copy in fetched(pairs, sems):
        copy.wait()
    at_belt = lax.axis_index("belt")
    wanted = peer_ref[jnp.where(first, 0, 1), at_belt ^ 1]
    pick_ref[...] = jnp.full(pick_ref.shape, jnp.where(wanted == at_belt, 1.0, 0.0), BF)
    top, bottom = slice(0, SUB), slice(rows - SUB, rows)

    def bands_of(whole):
        if halves == 1:
            return [jnp.where(first, whole[bottom], whole[top])]
        return [whole[bottom], whole[top]]

    pieces, tiles, rim_rows = [[] for _ in range(halves)], [], []
    for f in range(2 * levels):
        own_ref[rows * f : rows * (f + 1)] = wind_ref[f // levels, f % levels]
        whole = wind_ref[f // levels, f % levels].astype(F32)
        for k, band in enumerate(bands_of(whole)):
            pieces[k].append(band)
        tiles += [edge_tile(whole[r : r + SUB]) for r in range(0, rows, SUB)]
        rim_rows.append(jnp.where(first, whole[0:1], whole[rows - 1 : rows]))
    for q in range(3):
        for half, part in enumerate(split_hi_lo(kappa_ref[q] if q < 2 else metric_ref[...])):
            at = rows * (2 * levels + 2 * q + half)
            own_ref[at : at + rows] = part.astype(BF)
            for k, band in enumerate(bands_of(part)):
                pieces[k].append(band)
            tiles += [edge_tile(part[r : r + SUB]) for r in range(0, rows, SUB)]
    for k in range(halves):
        for i in range(0, len(pieces[k]), 2):
            both = jnp.concatenate([pieces[k][i], pieces[k][i + 1]], axis=0)
            both = both.astype(BF)
            for t in range(cols // LANES):
                part, at = bulk_place(t)
                ref = (bulk_0_ref, bulk_1_ref)[part]
                ref[k, SUB * i : SUB * (i + 2), at : at + LANES] = both[:, LANES * t : LANES * (t + 1)]
        for i, tile in enumerate(compact_rows([edge_tile(p) for p in pieces[k]])):
            corner_ref[k, :, LANES * i : LANES * (i + 1)] = tile
    rim = jnp.concatenate(rim_rows + [jnp.zeros((16 - len(rim_rows), cols), F32)], axis=0)
    rim_ref[...] = rim.astype(BF)
    side_ref[...] = jnp.zeros(side_ref.shape, BF)
    for i, tile in enumerate(compact_rows(tiles)):
        side_ref[:, LANES * i : LANES * (i + 1)] = tile
    if ends_col is not None:
        side_ref[:, ends_col : ends_col + LANES] = edge_tile(rim).astype(BF)


def rim_slot(block, at_belt, n_belt):
    if n_belt != 4:
        return block
    return jnp.where(block == at_belt, 0, jnp.where((block ^ at_belt) == 2, 2, 1))


def end_slot(block, at_belt, n_belt):
    if n_belt != 4:
        return block
    offset = block ^ at_belt
    return jnp.where(offset == 2, 3, jnp.where(offset == 3, 2, offset))


class Rows:
    def __init__(self, levels, rows, halves):
        self.levels, self.rows, self.halves = levels, rows, halves
        self.fields, self.bands = 2 * levels, 2 * levels + 6
        self.tiles, self.span = rows // SUB, SUB * halves
        self.slab = self.tiles + halves
        self.height = SUB * self.slab

    def own_base(self, f):
        return 2 * self.height * (f // 2) + (self.height + self.span) * (f % 2)

    def band_base(self, f):
        return 2 * self.height * (f // 2) + self.rows

    def place_of(self, f, e):
        return e if f % 2 == 0 else (e + self.halves) % self.slab


def east_of(f):
    return [f[1], f[2], pltpu.roll(f[0], LANES - 1, 1)]


def west_of(f):
    return [pltpu.roll(f[2], 1, 1), f[0], f[1]]


def fill_order(order_ref, source_of):
    size = order_ref.shape[0]
    at = lax.broadcasted_iota(jnp.int32, (size, LANES), 0)
    lane = lax.broadcasted_iota(jnp.int32, (1, LANES), 1)
    for r in range(3):
        tile = jnp.where(at == source_of(3 * lane + r), 1.0, 0.0).astype(BF)
        order_ref[:, LANES * r : LANES * (r + 1)] = tile
        order_ref[:, LANES * (3 + r) : LANES * (4 + r)] = tile


def solve_window(lay, first, last, x_ref, order_ref, work):
    y_ref, coef_ref, met_ref, even_ref, odd_ref, fin_ref, z_ref = work
    levels, rows, fields, tiles = lay.levels, lay.rows, lay.fields, lay.tiles
    slab, height, span = lay.slab, lay.height, lay.span
    sub = lax.broadcasted_iota(jnp.int32, (SUB, LANES), 0)
    sub_slab = lax.broadcasted_iota(jnp.int32, (height, LANES), 0)
    closed = ((sub_slab == rows - 1) & last) | ((sub_slab == height - 1) & first)

    def put(ref, f, r, i, value):
        ref[f, r, SUB * (i + 1) : SUB * (i + 2)] = value
        if i == 0:
            ref[f, r, SUB * (slab + 1) : SUB * (slab + 2)] = value
        if i == slab - 1:
            ref[f, r, 0:SUB] = value
        if r == 0:
            return [(ref, f, 3, i, pltpu.roll(value, LANES - 1, 1))]
        if r == 2:
            return [(ref, f, 4, i, pltpu.roll(value, 1, 1))]
        return []

    def flush(rotated):
        for ref, f, plane, i, value in rotated:
            ref[f, plane, SUB * (i + 1) : SUB * (i + 2)] = value

    def advance(source, target, final):
        waiting = []
        for c in range(2):
            for e in range(tiles if final else slab):
                mid, east, west, south, north = (
                    [coef_ref[c, k, r, SUB * e : SUB * (e + 1)] for r in range(3)] for k in range(5)
                )
                results = []
                for lev in range(levels):
                    f = c * levels + lev
                    at = SUB * (lay.place_of(f, e) + 1)
                    here = [source[f, r, at : at + SUB] for r in range(5)]
                    right, left = [here[1], here[2], here[3]], [here[4], here[0], here[1]]
                    results.append(
                        [
                            (mid[r] * here[r] + south[r] * source[f, r, at + 1 : at + 1 + SUB])
                            + north[r] * source[f, r, at - 1 : at - 1 + SUB]
                            + (east[r] * right[r] + west[r] * left[r])
                            for r in range(3)
                        ]
                    )
                rotated = []
                for lev in range(levels):
                    f = c * levels + lev
                    for r in range(3):
                        if final:
                            fin_ref[rows * f + SUB * e : rows * f + SUB * (e + 1), LANES * r : LANES * (r + 1)] = results[lev][r]
                        else:
                            rotated += put(target, f, r, lay.place_of(f, e), results[lev][r])
                flush(waiting)
                waiting = rotated
        flush(waiting)

    whole = jnp.dot(x_ref[...], order_ref[:, 0:WINDOW], preferred_element_type=F32)
    for r in range(3):
        y_ref[r] = whole[:, LANES * r : LANES * (r + 1)]
    for q in range(3):
        base = height * (fields + 2 * q)
        low = base + height
        value = [
            y_ref[r, base : base + height]
            + jnp.concatenate([y_ref[r, low + span : low + height], y_ref[r, low : low + span]], axis=0)
            for r in range(3)
        ]
        if q == 2:
            for r in range(3):
                met_ref[r] = 0.5 * value[r]
            continue
        right = east_of(value)
        east = [0.5 * (value[r] + right[r]) for r in range(3)]
        west = west_of(east)
        for r in range(3):
            south = jnp.where(closed, 0.0, 0.5 * (value[r] + pltpu.roll(value[r], height - 1, 0)))
            north = pltpu.roll(south, 1, 0)
            coef_ref[q, 0, r] = 1.0 - ((east[r] + west[r]) + (south + north))
            coef_ref[q, 1, r] = east[r]
            coef_ref[q, 2, r] = west[r]
            coef_ref[q, 3, r] = south
            coef_ref[q, 4, r] = north
    waiting = []
    for e in range(slab):
        rotated = []
        metric = [met_ref[r, SUB * e : SUB * (e + 1)] for r in range(3)]
        for lev in range(levels):
            across, belt = [], []
            for c in range(2):
                f = c * levels + lev
                base, i = height * f, lay.place_of(f, e)
                at = base + SUB * i
                here = [y_ref[r, at : at + SUB] for r in range(3)]
                right, left = east_of(here), west_of(here)
                belt.append([right[r] - left[r] for r in range(3)])
                diffs = []
                for r in range(3):
                    if i < slab - 1:
                        below = y_ref[r, at + 1 : at + 1 + SUB]
                    else:
                        wrap = pltpu.roll(y_ref[r, base : base + SUB], SUB - 1, 0)
                        below = jnp.where(sub == SUB - 1, wrap, pltpu.roll(here[r], SUB - 1, 0))
                    if i > 0:
                        above = y_ref[r, at - 1 : at - 1 + SUB]
                    else:
                        end = base + height
                        wrap = pltpu.roll(y_ref[r, end - SUB : end], 1, 0)
                        above = jnp.where(sub == 0, wrap, pltpu.roll(here[r], 1, 0))
                    diffs.append(below - above)
                across.append(diffs)
            for r in range(3):
                curl = metric[r] * (across[0][r] - belt[1][r])
                divergence = metric[r] * (-belt[0][r] - across[1][r])
                rotated += put(even_ref, lev, r, lay.place_of(lev, e), curl)
                rotated += put(even_ref, levels + lev, r, lay.place_of(levels + lev, e), divergence)
        flush(waiting)
        waiting = rotated
    flush(waiting)

    def two(k, _):
        advance(even_ref, odd_ref, False)
        advance(odd_ref, even_ref, False)
        return 0

    lax.fori_loop(0, STEPS // 2 - 1, two, 0)
    advance(even_ref, odd_ref, False)
    advance(odd_ref, None, True)
    value = fin_ref[...]
    hi = value.astype(BF)
    z_ref[:, 0 : 3 * LANES] = hi
    z_ref[:, 3 * LANES :] = (value - hi.astype(F32)).astype(BF)


def work_shapes(lay):
    return [
        pltpu.VMEM((3, lay.height * lay.bands, LANES), F32),
        pltpu.VMEM((2, 5, 3, lay.height, LANES), F32),
        pltpu.VMEM((3, lay.height, LANES), F32),
        pltpu.VMEM((lay.fields, 5, lay.height + 2 * SUB, LANES), F32),
        pltpu.VMEM((lay.fields, 5, lay.height + 2 * SUB, LANES), F32),
        pltpu.VMEM((lay.rows * lay.fields, WINDOW), F32),
        pltpu.VMEM((lay.rows * lay.fields, 2 * WINDOW), BF),
    ]


def back_to_natural(z, order, cols):
    return lax.dot_general(z, order[cols], (((1,), (1,)), ((), ())), preferred_element_type=F32)


def ghost_tile_at(lay, first):
    return pl.multiple_of(jnp.where(first, 0, lay.rows - SUB), SUB)


def middle_kernel(
    lay, tile, offset, keep, own_ref, bulk_0_ref, bulk_1_ref, pick_ref,
    out_ref, order_ref, coef_out, met_out, pick_out, x_ref, *work,
):
    pick_out[...] = pick_ref[...]
    first, last = lax.axis_index("across") == 0, lax.axis_index("across") == lax.axis_size("across") - 1
    cols = slice(LANES * tile, LANES * (tile + 4))
    fill_order(order_ref, lambda place: place + offset)
    for f in range(lay.bands):
        base = lay.own_base(f)
        x_ref[base : base + lay.rows] = own_ref[lay.rows * f : lay.rows * (f + 1), cols]
    span = lay.span
    at_row = lax.broadcasted_iota(jnp.int32, (2 * span, 4 * LANES), 0)
    for f in range(0, lay.bands, 2):
        band = bulk_tiles((bulk_0_ref, bulk_1_ref), span * f, 2 * span, range(tile, tile + 4))
        if f < lay.fields:
            band = band.astype(F32)
            for k in range(2):
                spot = jnp.where(first, span * (k + 1) - 1, jnp.where(last, span * k, -1))
                band = jnp.where(at_row == spot, 0.0, band)
            band = band.astype(BF)
        at = lay.band_base(f)
        x_ref[at : at + 2 * span] = band
    solve_window(lay, first, last, x_ref, order_ref, work)
    back = back_to_natural(work[-1][...], order_ref, slice(LANES * keep, LANES * (keep + 3)))
    for f in range(lay.fields):
        out_ref[f // lay.levels, f % lay.levels] = back[lay.rows * f : lay.rows * (f + 1)]
    at = ghost_tile_at(lay, first)
    coef_out[...] = work[1][:, :, :, pl.ds(at, SUB)]
    met_out[...] = work[2][:, pl.ds(at, SUB)]


def edge_kernel(lay, n_belt, relay, plan, peer_ref, flip_ref, turn_ref, own_ref, bulk_0_ref, bulk_1_ref, *rest):
    if relay is None:
        side_a_ref, side_b_ref, corner_a_ref, corner_b_ref, rims_ref, ends_ref, *rest = rest
    else:
        rim_ref, side_ref, far_ref, near_ref, *rest = rest
        *rest, rims_ref, ends_ref = rest
        corner_at, ends_at = relay
        side_a_ref, side_b_ref = near_ref.at[16:32], near_ref.at[32:48]
        corner_a_ref, corner_b_ref = (
            near_ref.at[pl.ds(k, 16), corner_at:ends_at] for k in (16, 32)
        )
        for k, rim in enumerate((rim_ref[...], near_ref[0:16], far_ref[0:16])):
            rims_ref[k] = rim
        ends_cols = slice(ends_at, ends_at + LANES)
        for k, (ref, at) in enumerate(((side_ref, 0), (near_ref, 16), (near_ref, 32), (far_ref, 16))):
            ends_ref[k] = ref[at : at + 16, ends_cols]
    middles, rest = [rest[4 * k : 4 * k + 4] for k in range(2)], rest[8:]
    out_hbm, x_ref, order_ref, ghost_ref, grow_ref, ext_ref, strip_ref, sems, *work = rest
    levels, rows, cols = lay.levels, lay.rows, own_ref.shape[1]
    tiles, halves, fields, bands, span = lay.tiles, lay.halves, lay.fields, lay.bands, lay.span
    at_belt, at_across = lax.axis_index("belt"), lax.axis_index("across")
    first, last = at_across == 0, at_across == lax.axis_size("across") - 1
    ghost_at = ghost_tile_at(lay, first)
    rest_at = pl.multiple_of(jnp.where(first, SUB, 0), SUB)
    calm = pl.ds(rest_at, rows - SUB)
    left_end, split, right_start, right_end = plan
    early = [
        pltpu.make_async_copy(
            middles[0][0].at[:, :, calm, LANES:], out_hbm.at[:, :, calm, left_end:split], sems.at[0]
        ),
        pltpu.make_async_copy(
            middles[1][0].at[:, :, calm, : 2 * LANES], out_hbm.at[:, :, calm, split:right_start], sems.at[1]
        ),
    ]
    for copy in early:
        copy.start()
    even = lax.rem(at_belt, 2) == 0
    from_right = (lane_iota() // 8) % 2 == 1
    take_a = from_right == even

    def unpacked(a_ref, b_ref, groups):
        out = []
        for g in range(groups):
            column, half = LANES * (g // 2), slice(SUB * (g % 2), SUB * (g % 2) + SUB)
            a = a_ref(column).astype(F32)[half]
            b = b_ref(column).astype(F32)[half]
            out.append(jnp.where(take_a, a, b))
        return out

    def put_back(packed, index):
        return pltpu.roll(packed[index // SLOTS], (-(8 + 16 * (index % SLOTS))) % LANES, 1)

    ghost_ref[...] = jnp.zeros(ghost_ref.shape, F32)
    edge = jnp.where(first, 0, 1)
    lane_r = lax.broadcasted_iota(jnp.int32, (LANES, LANES), 0)
    lane_c = lax.broadcasted_iota(jnp.int32, (LANES, LANES), 1)
    backward = jnp.where(lane_r + lane_c == LANES - 1, 1.0, 0.0).astype(BF)
    blocks = [at_belt, lax.rem(at_belt + 1, n_belt), lax.rem(at_belt + n_belt - 1, n_belt)]
    peers = [peer_ref[edge, block] for block in blocks]
    own_rim = rims_ref[rim_slot(peers[0], at_belt, n_belt)]
    col_tiles = cols // LANES
    raw = [own_rim[:, LANES * t : LANES * (t + 1)] for t in range(col_tiles)]
    raw += [ends_ref[end_slot(peer, at_belt, n_belt)] for peer in peers[1:]]
    turned = jnp.dot(jnp.concatenate(raw, axis=0), backward, preferred_element_type=F32)

    def ghost_parts(block, plain, flipped):
        flip, turn = flip_ref[edge, block], turn_ref[edge, block]
        found = jnp.where(flip == 1, turned[16 * flipped : 16 * (flipped + 1)], raw[plain].astype(F32))
        p, q = found[0:levels], found[levels : 2 * levels]
        cosine = jnp.where(turn == 0, 1.0, jnp.where(turn == 2, -1.0, 0.0))
        sine_neg = jnp.where(turn == 1, -1.0, jnp.where(turn == 3, 1.0, 0.0))
        return cosine * p + sine_neg * q, cosine * q - sine_neg * p

    for t in range(col_tiles):
        for c, part in enumerate(ghost_parts(blocks[0], t, col_tiles - 1 - t)):
            ghost_ref[c, 0:levels, LANES * t : LANES * (t + 1)] = part
    after_tiles = ghost_parts(blocks[1], col_tiles, col_tiles)
    before_tiles = ghost_parts(blocks[2], col_tiles + 1, col_tiles + 1)
    lane_row = lax.broadcasted_iota(jnp.int32, (levels, LANES), 1)
    for c in range(2):
        both = jnp.where(lane_row < LANES // 2, after_tiles[c], before_tiles[c])
        ghost_ref[c, 0:levels, cols:] = both

    side_tiles = unpacked(
        lambda k: side_a_ref[:, k : k + LANES], lambda k: side_b_ref[:, k : k + LANES],
        -(-bands * tiles // SLOTS),
    )
    corners = [
        unpacked(
            lambda k, at=at: (corner_a_ref if relay else corner_a_ref.at[at])[:, k : k + LANES],
            lambda k, at=at: (corner_b_ref if relay else corner_b_ref.at[at])[:, k : k + LANES],
            -(-bands // SLOTS),
        )
        for at in range(halves)
    ]
    near_start, near_end = slice(0, 2 * LANES), slice(cols - 2 * LANES, cols)
    for part, place in ((near_start, slice(LANES, 3 * LANES)), (near_end, slice(3 * LANES, 5 * LANES))):
        for f in range(bands):
            base = lay.own_base(f)
            x_ref[base : base + rows, place] = own_ref[rows * f : rows * (f + 1), part]
    for f in range(bands):
        halo = jnp.concatenate([put_back(side_tiles, f * tiles + r) for r in range(tiles)], axis=0)
        x_ref[lay.own_base(f) : lay.own_base(f) + rows, 0:LANES] = halo.astype(BF)
    at_row = lax.broadcasted_iota(jnp.int32, (2 * span, 5 * LANES), 0)
    for f in range(0, bands, 2):
        col_tiles = cols // LANES
        body = bulk_tiles(
            (bulk_0_ref, bulk_1_ref), span * f, 2 * span, (0, 1, col_tiles - 2, col_tiles - 1)
        ).astype(F32)
        halo = jnp.concatenate(
            [put_back(corners[at], f + k) for k in range(2) for at in range(halves)], axis=0
        )
        band = jnp.concatenate([halo, body], axis=1)
        if f < fields:
            for k in range(2):
                c, lev = (f + k) // levels, (f + k) % levels
                row = ghost_ref[c, lev : lev + 1, :]
                row = jnp.concatenate([row[:, cols:], row[:, near_start], row[:, near_end]], axis=1)
                spot = jnp.where(first, span * (k + 1) - 1, jnp.where(last, span * k, -1))
                band = jnp.where(at_row == spot, row, band)
        x_ref[lay.band_base(f) : lay.band_base(f) + 2 * span] = band.astype(BF)

    half, size = WINDOW // 2, 5 * LANES

    def source_of(place):
        at_left = place + LANES - MARGIN
        at_right = place + size - (WINDOW - MARGIN)
        return jnp.where(place < half, at_left, jnp.where(at_right < size, at_right, at_right - size))

    fill_order(order_ref, source_of)

    sub = lax.broadcasted_iota(jnp.int32, (SUB, LANES), 0)
    spot = jnp.where(first, 0, SUB - 1)
    sign = jnp.where(first, -1.0, jnp.where(last, 1.0, 0.0))
    lift = jnp.where(sub == spot, sign, 0.0)
    values = []
    for k, (_, order, coef, met) in enumerate(middles):
        cols_k = slice(LANES * MIDDLES[k][0], LANES * (MIDDLES[k][0] + 4))
        rows_k = jnp.concatenate([ghost_ref[0, :, cols_k], ghost_ref[1, :, cols_k]], axis=0).astype(BF)
        found = jnp.dot(rows_k, order[:, 0:WINDOW], preferred_element_type=F32)
        for f in range(fields):
            c, lev = f // levels, f % levels
            row = found[SUB * c + lev : SUB * c + lev + 1]
            scale = [(1.0 - 2.0 * c) * lift * met[r] for r in range(3)]
            values.append([scale[r] * row[:, LANES * r : LANES * (r + 1)] for r in range(3)])
    inner_south, inner_north = sub < SUB - 1, sub > 0
    for _ in range(STEPS):
        updated = []
        for at, f in enumerate(values):
            coef, c = middles[at // fields][2], at % fields // levels
            right, left = east_of(f), west_of(f)
            updated.append(
                [
                    (coef[c, 0, r] * f[r] + coef[c, 1, r] * right[r] + coef[c, 2, r] * left[r])
                    + jnp.where(inner_south, coef[c, 3, r], 0.0) * pltpu.roll(f[r], SUB - 1, 0)
                    + jnp.where(inner_north, coef[c, 4, r], 0.0) * pltpu.roll(f[r], 1, 0)
                    for r in range(3)
                ]
            )
        values = updated
    for at, f in enumerate(values):
        for r in range(3):
            grow_ref[SUB * at : SUB * (at + 1), LANES * r : LANES * (r + 1)] = f[r]
    strips = []
    for k in range(2):
        grown = grow_ref[SUB * fields * k : SUB * fields * (k + 1)]
        hi = grown.astype(BF)
        parts = jnp.concatenate([hi, (grown - hi.astype(F32)).astype(BF)], axis=1)
        keep = MIDDLES[k][2]
        strips.append(back_to_natural(parts, middles[k][1], slice(LANES * keep, LANES * (keep + 3))))
    for f in range(fields):
        c, lev = f // levels, f % levels
        for k, part in ((0, slice(LANES, WINDOW)), (1, slice(0, 2 * LANES))):
            added = strips[k][SUB * f : SUB * (f + 1), part]
            strip_ref[c, lev, :, 2 * LANES * k : 2 * LANES * (k + 1)] = (
                middles[k][0][c, lev, pl.ds(ghost_at, SUB), part] + added
            )
    edge_rows = pl.ds(ghost_at, SUB)
    strip_copy = pltpu.make_async_copy(
        strip_ref, out_hbm.at[:, :, edge_rows, left_end:right_start], sems.at[2]
    )
    strip_copy.start()

    solve_window(lay, first, last, x_ref, order_ref, work)
    back = back_to_natural(work[-1][...], order_ref, slice(LANES, 5 * LANES))
    lane = lax.broadcasted_iota(jnp.int32, (rows, LANES), 1)
    lane_tile = lane[:SUB]
    low, high = MIDDLE_FROM - LANES, right_end - right_start
    for f in range(fields):
        c, lev = f // levels, f % levels
        mine = back[rows * f : rows * (f + 1)]
        ext_ref[c, lev, :, 0:LANES] = mine[:, 0:LANES]
        ext_ref[c, lev, :, 3 * LANES :] = mine[:, 3 * LANES :]
        one, two = slice(LANES, 2 * LANES), slice(2 * LANES, 3 * LANES)
        ext_ref[c, lev, :, one] = jnp.where(lane < low, mine[:, one], middles[0][0][c, lev, :, 0:LANES])
        ext_ref[c, lev, :, two] = jnp.where(lane >= high, mine[:, two], middles[1][0][c, lev, :, 2 * LANES :])
        for k, (place, mask, part) in enumerate(
            ((one, lane_tile >= low, slice(0, LANES)), (two, lane_tile < high, slice(2 * LANES, WINDOW)))
        ):
            added = strips[k][SUB * f : SUB * (f + 1), part]
            ext_ref[c, lev, edge_rows, place] = ext_ref[c, lev, edge_rows, place] + jnp.where(mask, added, 0.0)
    late = [
        pltpu.make_async_copy(ext_ref.at[:, :, :, : 2 * LANES], out_hbm.at[:, :, :, :left_end], sems.at[3]),
        pltpu.make_async_copy(ext_ref.at[:, :, :, 2 * LANES :], out_hbm.at[:, :, :, right_start:], sems.at[4]),
    ]
    for copy in late:
        copy.start()
    for copy in early + [strip_copy] + late:
        copy.wait()


def per_device(wind, metric, kappa, edge_peer, edge_flip, edge_turn):
    _, levels, rows, cols = wind.shape
    n_across, n_belt = lax.axis_size("across"), lax.axis_size("belt")
    halves = 1 if n_across == 2 else 2
    fields = 2 * levels
    bands = fields + 6
    corner_cols = LANES * (-(-bands // (2 * SLOTS)))
    side_cols = LANES * (-(-bands * (rows // SUB) // (2 * SLOTS)))
    ends_col = side_cols + corner_cols
    relay = halves == 1 and n_belt == 4 and ends_col + LANES <= cols

    vmem = pl.BlockSpec(memory_space=pltpu.VMEM)
    smem = pl.BlockSpec(memory_space=pltpu.SMEM)
    anywhere = pl.BlockSpec(memory_space=pl.ANY)
    lay = Rows(levels, rows, halves)
    height, span = lay.height, lay.span
    bulk_0, bulk_1, corner, rim, side, own, pick = pl.pallas_call(
        functools.partial(pack_kernel, halves, ends_col if relay else None),
        out_shape=[
            jax.ShapeDtypeStruct((halves, SUB * bands, 4 * LANES), BF),
            jax.ShapeDtypeStruct((halves, SUB * bands, cols - 4 * LANES), BF),
            jax.ShapeDtypeStruct((halves, 16, corner_cols), BF),
            jax.ShapeDtypeStruct((16, cols), BF),
            jax.ShapeDtypeStruct((16, cols), BF),
            jax.ShapeDtypeStruct((rows * bands, cols), BF),
            jax.ShapeDtypeStruct((16, cols), BF),
        ],
        in_specs=[anywhere] * 4,
        out_specs=[vmem] * 7,
        scratch_shapes=[
            pltpu.VMEM(wind.shape, BF),
            pltpu.VMEM(kappa.shape, F32),
            pltpu.VMEM(metric.shape, F32),
            pltpu.SMEM(edge_peer.shape, jnp.int32),
            pltpu.SemaphoreType.DMA((4,)),
        ],
        compiler_params=pltpu.CompilerParams(vmem_limit_bytes=PACK_LIMIT),
        name="pack",
    )(*(pltpu.with_memory_space_constraint(x, pltpu.HBM) for x in (wind, metric, kappa, edge_peer)))

    pairs_a = [(i, i ^ 1) for i in range(n_belt)]
    pairs_b = [(i, (i + 1) % n_belt if i % 2 else (i - 1) % n_belt) for i in range(n_belt)]
    if halves == 1:
        swap = [(0, 1), (1, 0)]
        bulk_0, bulk_1, corner_in = (lax.ppermute(x, "across", swap) for x in (bulk_0, bulk_1, corner))
    else:
        onward = [(i, i + 1) for i in range(n_across - 1)]
        back = [(i + 1, i) for i in range(n_across - 1)]

        def both_ways(message):
            return jnp.stack(
                [
                    lax.ppermute(message[1], "across", back),
                    lax.ppermute(message[0], "across", onward),
                ]
            )

        bulk_0, bulk_1, corner_in = both_ways(bulk_0), both_ways(bulk_1), both_ways(corner)
    bulk_0, bulk_1 = (
        x.reshape(halves, bands, SUB, x.shape[-1]).swapaxes(0, 1).reshape(bands * span, x.shape[-1])
        for x in (bulk_0, bulk_1)
    )

    def middle(k, pick):
        tile, offset, keep = MIDDLES[k]
        inputs = (own, bulk_0, bulk_0 if k == 0 else bulk_1, pick)
        shapes = [
            jax.ShapeDtypeStruct((2, levels, rows, WINDOW), F32),
            jax.ShapeDtypeStruct((4 * LANES, 2 * WINDOW), BF),
            jax.ShapeDtypeStruct((2, 5, 3, SUB, LANES), F32),
            jax.ShapeDtypeStruct((3, SUB, LANES), F32),
            jax.ShapeDtypeStruct(pick.shape, BF),
        ]
        return pl.pallas_call(
            functools.partial(middle_kernel, lay, tile, offset, keep),
            out_shape=shapes,
            in_specs=[vmem] * len(inputs),
            out_specs=[vmem] * len(shapes),
            scratch_shapes=[pltpu.VMEM((height * bands, 4 * LANES), BF)] + work_shapes(lay),
            compiler_params=pltpu.CompilerParams(vmem_limit_bytes=MID_LIMIT),
            cost_estimate=pl.CostEstimate(flops=2_000_000_000, bytes_accessed=2_000_000, transcendentals=0),
            name="middle",
        )(*inputs)

    if relay:
        spot = slice(side_cols, ends_col)
        side = jnp.concatenate([side[:, :side_cols], corner_in[0], side[:, ends_col:]], axis=1)
        *middle_0, pick = middle(0, pick)
        far = lax.ppermute(jnp.concatenate([rim, side]), "belt", [(i, i ^ 2) for i in range(n_belt)])
        rim_c, side_c = far[:16], far[16:]
        chosen = jnp.where(pick > 0, rim, rim_c)
        near = lax.ppermute(jnp.concatenate([chosen, side, side_c]), "belt", pairs_a)
        *middle_1, _ = middle(1, pick)
        messages = [rim, side, far, near]
    else:
        side_a = lax.ppermute(side, "belt", pairs_a)
        side_b = lax.ppermute(side, "belt", pairs_b)
        corner_a = lax.ppermute(corner_in, "belt", pairs_a)
        corner_b = lax.ppermute(corner_in, "belt", pairs_b)
        rims = lax.all_gather(rim, "belt")
        if n_belt == 4:
            at_belt = lax.axis_index("belt")
            rims, ends = (rims[at_belt ^ jnp.array([0, 1, 2])], rims[at_belt ^ jnp.array([0, 1, 3, 2])])
        else:
            ends = rims
        ends = jnp.concatenate([ends[..., : LANES // 2], ends[..., cols - LANES // 2 :]], axis=-1)

        messages = [side_a, side_b, corner_a, corner_b, rims, ends]
        (*middle_0, _), (*middle_1, _) = middle(0, pick), middle(1, pick)
    operands = [own, bulk_0, bulk_1, *messages, *middle_0, *middle_1]
    own_rims = [pltpu.VMEM((3, 16, cols), BF), pltpu.VMEM((4, 16, LANES), BF)] if relay else []
    plan = (2 * LANES, cols // 2, cols - 2 * LANES, MIDDLE_TO)
    return pl.pallas_call(
        functools.partial(edge_kernel, lay, n_belt, (side_cols, ends_col) if relay else None, plan),
        out_shape=jax.ShapeDtypeStruct((2, levels, rows, cols), F32),
        in_specs=[smem] * 3 + [vmem] * len(operands),
        out_specs=anywhere,
        scratch_shapes=[
            pltpu.VMEM((height * bands, 5 * LANES), BF),
            pltpu.VMEM((5 * LANES, 2 * WINDOW), BF),
            pltpu.VMEM((2, SUB, cols + LANES), F32),
            pltpu.VMEM((2 * fields * SUB, WINDOW), F32),
            pltpu.VMEM((2, levels, rows, 4 * LANES), F32),
            pltpu.VMEM((2, levels, SUB, 4 * LANES), F32),
            pltpu.SemaphoreType.DMA((5,)),
        ]
        + work_shapes(lay)
        + own_rims,
        compiler_params=pltpu.CompilerParams(vmem_limit_bytes=EDGE_LIMIT),
        name="edges",
    )(edge_peer, edge_flip, edge_turn, *operands)


def solution(mesh):
    return jax.shard_map(
        per_device,
        mesh=mesh,
        in_specs=(
            P(None, ("members", "lev"), "across", "belt"),
            P("across", "belt"),
            P(None, "across", "belt"),
            P(),
            P(),
            P(),
        ),
        out_specs=P(None, ("members", "lev"), "across", "belt"),
        check_vma=False,
    )
```

```python
import functools

import jax
import jax.numpy as jnp
import numpy as np
from jax import lax
from jax.experimental import pallas as pl
from jax.experimental.pallas import tpu as pltpu
from jax.sharding import PartitionSpec as P

STEPS = 6
LANES = 128
SUB = 8
SLOTS = 8
BF = jnp.bfloat16
F32 = jnp.float32
MARGIN = STEPS + 1
PARTS = 4
WINDOW = PARTS * LANES
PACK_LIMIT = 8 << 20
MID_LIMIT = 20 << 20
EDGE_LIMIT = 20 << 20


def split_hi_lo(value):
    hi = value.astype(BF).astype(F32)
    return hi, value - hi


def lane_iota():
    return lax.broadcasted_iota(jnp.int32, (SUB, LANES), 1)


def sub_iota(width):
    return lax.broadcasted_iota(jnp.int32, (SUB, width), 0)


def compact(tiles):
    slot = lane_iota() // 16
    packed = []
    for at in range(0, len(tiles), SLOTS):
        total = None
        for g, tile in enumerate(tiles[at : at + SLOTS]):
            moved = pltpu.roll(tile, (8 + 16 * g) % LANES, 1)
            total = moved if total is None else jnp.where(slot == g, moved, total)
        packed.append(total)
    return packed


def fetched(pairs, sems):
    copies = [pltpu.make_async_copy(src, dst, sems.at[i]) for i, (src, dst) in enumerate(pairs)]
    for copy in copies:
        copy.start()
    return copies


def edge_tile(band):
    left = lax.broadcasted_iota(jnp.int32, (band.shape[0], LANES), 1) < LANES // 2
    return jnp.where(left, band[:, :LANES], band[:, band.shape[1] - LANES :])


def compact_rows(tiles):
    packed = compact(tiles)
    packed += [jnp.zeros((SUB, LANES), F32)] * (-len(packed) % 2)
    return [jnp.concatenate(packed[i : i + 2], axis=0).astype(BF) for i in range(0, len(packed), 2)]


def pack_kernel(
    halves, ends_col, n_belt, wind_hbm, metric_hbm, kappa_hbm, peer_hbm, flip_hbm, turn_hbm,
    bulk_ref, corner_ref, rim_ref, side_ref, own_ref, pick_ref, facts_ref, *scratch
):
    wind_ref, kappa_ref, metric_ref, peer_ref, flip_ref, turn_ref, sems = scratch
    levels, rows, cols = wind_hbm.shape[1:]
    first = lax.axis_index("across") == 0
    pairs = [(wind_hbm, wind_ref), (kappa_hbm, kappa_ref), (metric_hbm, metric_ref)]
    pairs += [(peer_hbm, peer_ref), (flip_hbm, flip_ref), (turn_hbm, turn_ref)]
    for copy in fetched(pairs, sems):
        copy.wait()
    at_belt = lax.axis_index("belt")
    edge = jnp.where(first, 0, 1)
    for i, block in enumerate((at_belt, lax.rem(at_belt + 1, n_belt), lax.rem(at_belt + n_belt - 1, n_belt))):
        slot = (end_slot if i else rim_slot)(peer_ref[edge, block], at_belt, n_belt)
        turn = turn_ref[edge, block]
        cosine = jnp.where(turn == 0, 1.0, jnp.where(turn == 2, -1.0, 0.0))
        sine_neg = jnp.where(turn == 1, -1.0, jnp.where(turn == 3, 1.0, 0.0))
        found = (slot.astype(F32), flip_ref[edge, block].astype(F32), cosine, sine_neg)
        for k, value in enumerate(found):
            facts_ref[4 * i + k] = jnp.full((16, LANES), value, F32)
    wanted = peer_ref[edge, at_belt ^ 1]
    pick_ref[...] = jnp.full(pick_ref.shape, jnp.where(wanted == at_belt, 1.0, 0.0), BF)
    top, bottom = slice(0, SUB), slice(rows - SUB, rows)

    def bands_of(whole):
        if halves == 1:
            return [jnp.where(first, whole[bottom], whole[top])]
        return [whole[bottom], whole[top]]

    pieces, tiles, rim_rows = [[] for _ in range(halves)], [], []
    for f in range(2 * levels):
        own_ref[rows * f : rows * (f + 1)] = wind_ref[f // levels, f % levels]
        whole = wind_ref[f // levels, f % levels].astype(F32)
        for k, band in enumerate(bands_of(whole)):
            pieces[k].append(band)
        tiles += [edge_tile(whole[r : r + SUB]) for r in range(0, rows, SUB)]
        rim_rows.append(jnp.where(first, whole[0:1], whole[rows - 1 : rows]))
    for q in range(3):
        for half, part in enumerate(split_hi_lo(kappa_ref[q] if q < 2 else metric_ref[...])):
            at = rows * (2 * levels + 2 * q + half)
            own_ref[at : at + rows] = part.astype(BF)
            for k, band in enumerate(bands_of(part)):
                pieces[k].append(band)
            tiles += [edge_tile(part[r : r + SUB]) for r in range(0, rows, SUB)]
    for k in range(halves):
        for i in range(0, len(pieces[k]), 2):
            both = jnp.concatenate([pieces[k][i], pieces[k][i + 1]], axis=0)
            bulk_ref[k, SUB * i : SUB * (i + 2)] = both.astype(BF)
        for i, tile in enumerate(compact_rows([edge_tile(p) for p in pieces[k]])):
            corner_ref[k, :, LANES * i : LANES * (i + 1)] = tile
    rim = jnp.concatenate(rim_rows + [jnp.zeros((16 - len(rim_rows), cols), F32)], axis=0)
    rim_ref[...] = rim.astype(BF)
    side_ref[...] = jnp.zeros(side_ref.shape, BF)
    for i, tile in enumerate(compact_rows(tiles)):
        side_ref[:, LANES * i : LANES * (i + 1)] = tile
    if ends_col is not None:
        side_ref[:, ends_col : ends_col + LANES] = edge_tile(rim).astype(BF)


def rim_slot(block, at_belt, n_belt):
    if n_belt != 4:
        return block
    return jnp.where(block == at_belt, 0, jnp.where((block ^ at_belt) == 2, 2, 1))


def end_slot(block, at_belt, n_belt):
    if n_belt != 4:
        return block
    offset = block ^ at_belt
    return jnp.where(offset == 2, 3, jnp.where(offset == 3, 2, offset))


class Rows:
    def __init__(self, levels, rows, halves):
        self.levels, self.rows, self.halves = levels, rows, halves
        self.fields, self.bands = 2 * levels, 2 * levels + 6
        self.tiles, self.span = rows // SUB, SUB * halves
        self.slab = self.tiles + halves
        self.height = SUB * self.slab

    def own_base(self, f):
        return 2 * self.height * (f // 2) + (self.height + self.span) * (f % 2)

    def band_base(self, f):
        return 2 * self.height * (f // 2) + self.rows

    def place_of(self, f, e):
        return e if f % 2 == 0 else (e + self.halves) % self.slab


def east_of(f):
    return [*f[1:], pltpu.roll(f[0], LANES - 1, 1)]


def west_of(f):
    return [pltpu.roll(f[-1], 1, 1), *f[:-1]]


def fill_order(order_ref, offset):
    size = order_ref.shape[0]
    at = lax.broadcasted_iota(jnp.int32, (size, LANES), 0)
    lane = lax.broadcasted_iota(jnp.int32, (1, LANES), 1)
    for r in range(PARTS):
        tile = jnp.where(at == PARTS * lane + (r + offset), 1.0, 0.0).astype(BF)
        order_ref[:, LANES * r : LANES * (r + 1)] = tile
        order_ref[:, LANES * (PARTS + r) : LANES * (PARTS + r + 1)] = tile


def solve_window(lay, first, last, x_ref, order_ref, work, extra=None):
    y_ref, coef_ref, met_ref, even_ref, odd_ref, fin_ref, z_ref = work
    levels, rows, fields, tiles = lay.levels, lay.rows, lay.fields, lay.tiles
    slab, height, span = lay.slab, lay.height, lay.span
    sub = lax.broadcasted_iota(jnp.int32, (SUB, LANES), 0)
    sub_slab = lax.broadcasted_iota(jnp.int32, (height, LANES), 0)
    closed = ((sub_slab == rows - 1) & last) | ((sub_slab == height - 1) & first)

    def put(ref, f, r, i, value):
        ref[f, r, SUB * (i + 1) : SUB * (i + 2)] = value
        if i == 0:
            ref[f, r, SUB * (slab + 1) : SUB * (slab + 2)] = value
        if i == slab - 1:
            ref[f, r, 0:SUB] = value
        if r == 0:
            return [(ref, f, PARTS, i, pltpu.roll(value, LANES - 1, 1))]
        if r == PARTS - 1:
            return [(ref, f, PARTS + 1, i, pltpu.roll(value, 1, 1))]
        return []

    def flush(rotated):
        for ref, f, plane, i, value in rotated:
            ref[f, plane, SUB * (i + 1) : SUB * (i + 2)] = value

    extra_place = slab + 2

    def advance(source, target, final):
        waiting = []
        for c in range(2):
            for e in [*range(tiles if final else slab)] + [None] * (extra is not None):
                mid, east, west, south, north = (
                    [
                        extra[0][c, k, r] if e is None else coef_ref[c, k, r, SUB * e : SUB * (e + 1)]
                        for r in range(PARTS)
                    ]
                    for k in range(5)
                )

                def place(f, e=e):
                    return extra_place if e is None else lay.place_of(f, e)

                results = []
                for lev in range(levels):
                    f = c * levels + lev
                    at = SUB * (place(f) + 1)
                    here = [source[f, r, at : at + SUB] for r in range(PARTS + 2)]
                    right = here[1 : PARTS + 1]
                    left = [here[PARTS + 1], *here[: PARTS - 1]]
                    results.append(
                        [
                            (mid[r] * here[r] + south[r] * source[f, r, at + 1 : at + 1 + SUB])
                            + north[r] * source[f, r, at - 1 : at - 1 + SUB]
                            + (east[r] * right[r] + west[r] * left[r])
                            for r in range(PARTS)
                        ]
                    )
                rotated = []
                for lev in range(levels):
                    f = c * levels + lev
                    for r in range(PARTS):
                        if final:
                            at = rows * fields + SUB * f if e is None else rows * f + SUB * e
                            fin_ref[at : at + SUB, LANES * r : LANES * (r + 1)] = results[lev][r]
                        else:
                            rotated += put(target, f, r, place(f), results[lev][r])
                flush(waiting)
                waiting = rotated
        flush(waiting)

    whole = jnp.dot(x_ref[...], order_ref[:, 0:WINDOW], preferred_element_type=F32)
    for r in range(PARTS):
        y_ref[r] = whole[:, LANES * r : LANES * (r + 1)]
    for q in range(3):
        base = height * (fields + 2 * q)
        low = base + height
        value = [
            y_ref[r, base : base + height]
            + jnp.concatenate([y_ref[r, low + span : low + height], y_ref[r, low : low + span]], axis=0)
            for r in range(PARTS)
        ]
        if q == 2:
            for r in range(PARTS):
                met_ref[r] = 0.5 * value[r]
            continue
        right = east_of(value)
        east = [0.5 * (value[r] + right[r]) for r in range(PARTS)]
        west = west_of(east)
        for r in range(PARTS):
            south = jnp.where(closed, 0.0, 0.5 * (value[r] + pltpu.roll(value[r], height - 1, 0)))
            north = pltpu.roll(south, 1, 0)
            coef_ref[q, 0, r] = 1.0 - ((east[r] + west[r]) + (south + north))
            coef_ref[q, 1, r] = east[r]
            coef_ref[q, 2, r] = west[r]
            coef_ref[q, 3, r] = south
            coef_ref[q, 4, r] = north
    waiting = []
    for e in range(slab):
        rotated = []
        metric = [met_ref[r, SUB * e : SUB * (e + 1)] for r in range(PARTS)]
        for lev in range(levels):
            across, belt = [], []
            for c in range(2):
                f = c * levels + lev
                base, i = height * f, lay.place_of(f, e)
                at = base + SUB * i
                here = [y_ref[r, at : at + SUB] for r in range(PARTS)]
                right, left = east_of(here), west_of(here)
                belt.append([right[r] - left[r] for r in range(PARTS)])
                diffs = []
                for r in range(PARTS):
                    if i < slab - 1:
                        below = y_ref[r, at + 1 : at + 1 + SUB]
                    else:
                        wrap = pltpu.roll(y_ref[r, base : base + SUB], SUB - 1, 0)
                        below = jnp.where(sub == SUB - 1, wrap, pltpu.roll(here[r], SUB - 1, 0))
                    if i > 0:
                        above = y_ref[r, at - 1 : at - 1 + SUB]
                    else:
                        end = base + height
                        wrap = pltpu.roll(y_ref[r, end - SUB : end], 1, 0)
                        above = jnp.where(sub == 0, wrap, pltpu.roll(here[r], 1, 0))
                    diffs.append(below - above)
                across.append(diffs)
            for r in range(PARTS):
                curl = metric[r] * (across[0][r] - belt[1][r])
                divergence = metric[r] * (-belt[0][r] - across[1][r])
                rotated += put(even_ref, lev, r, lay.place_of(lev, e), curl)
                rotated += put(even_ref, levels + lev, r, lay.place_of(levels + lev, e), divergence)
        flush(waiting)
        waiting = rotated
    flush(waiting)

    if extra is not None:
        for ref in (even_ref, odd_ref):
            for at in (extra_place, extra_place + 2):
                ref[:, 0:PARTS, SUB * at : SUB * (at + 1)] = jnp.zeros((fields, PARTS, SUB, LANES), F32)
        rotated = []
        for f in range(fields):
            c, lev = f // levels, f % levels
            at = height * lay.bands + SUB * c + lev
            for r in range(PARTS):
                value = (1.0 - 2.0 * c) * extra[1][r] * y_ref[r, at : at + 1]
                rotated += put(even_ref, f, r, extra_place, value)
        flush(rotated)

    def two(k, _):
        advance(even_ref, odd_ref, False)
        advance(odd_ref, even_ref, False)
        return 0

    lax.fori_loop(0, STEPS // 2 - 1, two, 0)
    advance(even_ref, odd_ref, False)
    advance(odd_ref, None, True)
    value = fin_ref[...]
    hi = value.astype(BF)
    z_ref[:, 0:WINDOW] = hi
    z_ref[:, WINDOW:] = (value - hi.astype(F32)).astype(BF)


def work_shapes(lay, extra):
    out_rows = (lay.rows + SUB * extra) * lay.fields
    plane = (lay.fields, PARTS + 2, lay.height + 2 * SUB + 3 * SUB * extra, LANES)
    return [
        pltpu.VMEM((PARTS, lay.height * lay.bands + 2 * SUB * extra, LANES), F32),
        pltpu.VMEM((2, 5, PARTS, lay.height, LANES), F32),
        pltpu.VMEM((PARTS, lay.height, LANES), F32),
        pltpu.VMEM(plane, F32),
        pltpu.VMEM(plane, F32),
        pltpu.VMEM((out_rows, WINDOW), F32),
        pltpu.VMEM((out_rows, 2 * WINDOW), BF),
    ]


def back_to_natural(z, order):
    return lax.dot_general(z, order, (((1,), (1,)), ((), ())), preferred_element_type=F32)


def ghost_tile_at(lay, first):
    return pl.multiple_of(jnp.where(first, 0, lay.rows - SUB), SUB)


def collect_rims(relay, refs, rims_ref, ends_ref):
    rim_ref, side_ref, far_ref, near_ref = refs
    for k, rim in enumerate((rim_ref[...], near_ref[0:16], far_ref[0:16])):
        rims_ref[k] = rim
    ends_cols = slice(relay[1], relay[1] + LANES)
    for k, (ref, at) in enumerate(((side_ref, 0), (near_ref, 16), (near_ref, 32), (far_ref, 16))):
        ends_ref[k] = ref[at : at + 16, ends_cols]


def ghost_rows(lay, facts_ref, rims_ref, ends_ref, ghost_ref):
    levels, cols = lay.levels, rims_ref.shape[-1]
    col_tiles = cols // LANES
    ghost_ref[...] = jnp.zeros(ghost_ref.shape, F32)

    def selected(i, ref, place):
        found = ref[0, :, place].astype(F32)
        for q in range(1, ref.shape[0]):
            found = jnp.where(facts_ref[4 * i] == q, ref[q, :, place].astype(F32), found)
        return found

    raw = [selected(0, rims_ref, slice(LANES * t, LANES * (t + 1))) for t in range(col_tiles)]
    raw += [selected(i, ends_ref, slice(0, LANES)) for i in (1, 2)]
    lane_r = lax.broadcasted_iota(jnp.int32, (LANES, LANES), 0)
    lane_c = lax.broadcasted_iota(jnp.int32, (LANES, LANES), 1)
    backward = jnp.where(lane_r + lane_c == LANES - 1, 1.0, 0.0).astype(BF)
    turned = reorder(jnp.concatenate(raw, axis=0).astype(BF), backward)

    def ghost_parts(i, plain, flipped):
        found = jnp.where(facts_ref[4 * i + 1] == 1, turned[16 * flipped : 16 * (flipped + 1)], raw[plain])
        p, q = found[0:levels], found[levels : 2 * levels]
        cosine, sine_neg = facts_ref[4 * i + 2, 0:levels], facts_ref[4 * i + 3, 0:levels]
        return cosine * p + sine_neg * q, cosine * q - sine_neg * p

    for t in range(col_tiles):
        for c, part in enumerate(ghost_parts(0, t, col_tiles - 1 - t)):
            ghost_ref[c, 0:levels, LANES * t : LANES * (t + 1)] = part
    after_tiles = ghost_parts(1, col_tiles, col_tiles)
    before_tiles = ghost_parts(2, col_tiles + 1, col_tiles + 1)
    lane_row = lax.broadcasted_iota(jnp.int32, (levels, LANES), 1)
    for c in range(2):
        both = jnp.where(lane_row < LANES // 2, after_tiles[c], before_tiles[c])
        ghost_ref[c, 0:levels, cols:] = both


def reorder(rows, order):
    return jnp.dot(rows, order, preferred_element_type=F32)


def middle_kernel(lay, k, relay, own_ref, bulk_ref, *rest):
    first, last = lax.axis_index("across") == 0, lax.axis_index("across") == lax.axis_size("across") - 1
    ghost_ref = None
    if k == 1:
        order_ref, weights_ref, touched_ref, facts_ref, *rest = rest
        if relay is None:
            rims_ref, ends_ref, out_ref, ghost_ref, grown_ref, x_ref, *work = rest
        else:
            *rest, rims_ref, ends_ref = rest
            collect_rims(relay, rest[:4], rims_ref, ends_ref)
            out_ref, ghost_ref, grown_ref, x_ref, *work = rest[4:]
        ghost_rows(lay, facts_ref, rims_ref, ends_ref, ghost_ref)
    else:
        out_ref, order_ref, weights_ref, touched_ref, x_ref, *work = rest
        fill_order(order_ref, 0)
    cols = slice(WINDOW * k, WINDOW * (k + 1))
    for f in range(lay.bands):
        base = lay.own_base(f)
        x_ref[base : base + lay.rows] = own_ref[lay.rows * f : lay.rows * (f + 1), cols]
    span = lay.span
    at_row = lax.broadcasted_iota(jnp.int32, (2 * span, WINDOW), 0)
    for f in range(0, lay.bands, 2):
        band = bulk_ref[span * f : span * (f + 2), cols]
        if f < lay.fields:
            band = band.astype(F32)
            for g in range(2):
                c, lev = (f + g) // lay.levels, (f + g) % lay.levels
                row = 0.0 if ghost_ref is None else ghost_ref[c, lev : lev + 1, cols]
                spot = jnp.where(first, span * (g + 1) - 1, jnp.where(last, span * g, -1))
                band = jnp.where(at_row == spot, row, band)
            band = band.astype(BF)
        at = lay.band_base(f)
        x_ref[at : at + 2 * span] = band
    extra = None
    if k == 1:
        beside = jnp.concatenate([ghost_ref[c, :, :WINDOW] for c in range(2)], axis=0)
        x_ref[lay.height * lay.bands :] = beside.astype(BF)
        sub = lax.broadcasted_iota(jnp.int32, (SUB, LANES), 0)
        sign = jnp.where(first, -1.0, jnp.where(last, 1.0, 0.0))
        lift = jnp.where(sub == jnp.where(first, 0, SUB - 1), sign, 0.0)
        extra = weights_ref, [lift * touched_ref[r] for r in range(PARTS)]
    solve_window(lay, first, last, x_ref, order_ref, work, extra)
    back = back_to_natural(work[-1][...], order_ref[...])
    for f in range(lay.fields):
        c, lev = f // lay.levels, f % lay.levels
        out_ref[c, lev] = back[lay.rows * f : lay.rows * (f + 1)]
        if k == 1:
            at = lay.rows * lay.fields + SUB * f
            grown_ref[c, lev] = back[at : at + SUB]
    if k == 0:
        at = ghost_tile_at(lay, first)
        weights_ref[...] = work[1][:, :, :, pl.ds(at, SUB)]
        touched_ref[...] = work[2][:, pl.ds(at, SUB)]


def weights(kappa, closed_rows):
    height, width = kappa.shape
    east = 0.5 * (kappa + pltpu.roll(kappa, width - 1, 1))
    west = pltpu.roll(east, 1, 1)
    south = jnp.where(closed_rows, 0.0, 0.5 * (kappa + pltpu.roll(kappa, height - 1, 0)))
    north = pltpu.roll(south, 1, 0)
    return 1.0 - ((east + west) + (south + north)), east, west, south, north


def diffused(values, coefs):
    def step(f, mid, east, west, south, north):
        height, width = f.shape
        return (mid * f + east * pltpu.roll(f, width - 1, 1) + west * pltpu.roll(f, 1, 1)) + (
            south * pltpu.roll(f, height - 1, 0) + north * pltpu.roll(f, 1, 0)
        )

    for _ in range(STEPS):
        values = [[step(f, *coef) for f in component] for component, coef in zip(values, coefs)]
    return values


def edge_kernel(lay, relay, own_ref, bulk_ref, ghost_ref, grown_ref, m0_ref, m1_ref, *rest):
    if relay is None:
        side_a_ref, side_b_ref, corner_a_ref, corner_b_ref, *rest = rest
    else:
        near_ref, *rest = rest
        side_a_ref, side_b_ref = near_ref.at[16:32], near_ref.at[32:48]
        corner_a_ref, corner_b_ref = (near_ref.at[pl.ds(k, 16), relay[0] : relay[1]] for k in (16, 32))
    out_hbm, head_ref, seam_ref, tail_ref, strip_ref, sems = rest
    levels, rows, cols = lay.levels, lay.rows, own_ref.shape[1]
    tiles, halves, fields, bands, span = lay.tiles, lay.halves, lay.fields, lay.bands, lay.span
    at_belt, at_across = lax.axis_index("belt"), lax.axis_index("across")
    first, last = at_across == 0, at_across == lax.axis_size("across") - 1
    ghost_at = ghost_tile_at(lay, first)
    edge_rows = pl.ds(ghost_at, SUB)
    calm = pl.ds(pl.multiple_of(jnp.where(first, SUB, 0), SUB), rows - SUB)
    inner, after = slice(LANES, WINDOW - LANES), slice(WINDOW + LANES, cols - LANES)
    early = [
        pltpu.make_async_copy(m0_ref.at[:, :, calm, inner], out_hbm.at[:, :, calm, inner], sems.at[0]),
        pltpu.make_async_copy(m1_ref.at[:, :, :, inner], out_hbm.at[:, :, :, after], sems.at[1]),
    ]
    for copy in early:
        copy.start()
    even = lax.rem(at_belt, 2) == 0
    from_right = (lane_iota() // 8) % 2 == 1
    take_a = from_right == even

    def unpacked(a_ref, b_ref, groups):
        out = []
        for g in range(groups):
            column, half = LANES * (g // 2), slice(SUB * (g % 2), SUB * (g % 2) + SUB)
            a = a_ref(column).astype(F32)[half]
            b = b_ref(column).astype(F32)[half]
            out.append(jnp.where(take_a, a, b))
        return out

    def put_back(packed, index):
        return pltpu.roll(packed[index // SLOTS], (-(8 + 16 * (index % SLOTS))) % LANES, 1)

    side_tiles = unpacked(
        lambda k: side_a_ref[:, k : k + LANES], lambda k: side_b_ref[:, k : k + LANES],
        -(-bands * tiles // SLOTS),
    )
    corners = [
        unpacked(
            lambda k, at=at: (corner_a_ref if relay else corner_a_ref.at[at])[:, k : k + LANES],
            lambda k, at=at: (corner_b_ref if relay else corner_b_ref.at[at])[:, k : k + LANES],
            -(-bands // SLOTS),
        )
        for at in range(halves)
    ]

    places = [slice(at, at + LANES) for at in (0, WINDOW - LANES, WINDOW, cols - LANES)]

    def fold(rows_of, halo):
        lane = lax.broadcasted_iota(jnp.int32, halo.shape, 1)
        start, before_seam, after_seam, end = (rows_of(place) for place in places)
        left = pltpu.roll(jnp.where(lane >= LANES - SUB, halo, start), SUB, 1)
        seam = pltpu.roll(jnp.where(lane >= LANES // 2, before_seam, after_seam), LANES // 2, 1)
        right = pltpu.roll(jnp.where(lane < SUB, halo, end), LANES - SUB, 1)
        return jnp.where(lane < 40, left, jnp.where(lane < 88, seam, right))

    ghosts = [fold(lambda place, c=c: ghost_ref[c, :, place], ghost_ref[c, :, cols:]) for c in range(2)]
    at_band = lax.broadcasted_iota(jnp.int32, (span, LANES), 0)
    spot = jnp.where(first, span - 1, jnp.where(last, 0, -1))
    slabs = []
    for f in range(bands):
        own = slice(rows * f, rows * (f + 1))
        halo = jnp.concatenate([put_back(side_tiles, f * tiles + r) for r in range(tiles)], axis=0)
        own_rows = fold(lambda place, own=own: own_ref[own, place].astype(F32), halo)
        pair, half = slice(span * (f - f % 2), span * (f - f % 2 + 2)), slice(span * (f % 2), span * (f % 2 + 1))
        band = fold(
            lambda place, pair=pair, half=half: bulk_ref[pair, place].astype(F32)[half],
            jnp.concatenate([put_back(corners[at], f) for at in range(halves)], axis=0),
        )
        if f < fields:
            c, lev = f // levels, f % levels
            band = jnp.where(at_band == spot, ghosts[c][lev : lev + 1], band)
        slabs.append(jnp.concatenate([own_rows, band], axis=0))
    at_row = lax.broadcasted_iota(jnp.int32, (lay.height, LANES), 0)
    closed = ((at_row == rows - 1) & last) | ((at_row == lay.height - 1) & first)
    kappas = [slabs[fields + 2 * q] + slabs[fields + 2 * q + 1] for q in range(3)]
    metric = 0.5 * kappas[2]

    def across_diff(f):
        return pltpu.roll(f, lay.height - 1, 0) - pltpu.roll(f, 1, 0)

    def belt_diff(f):
        return pltpu.roll(f, LANES - 1, 1) - pltpu.roll(f, 1, 1)

    pairs = [(slabs[lev], slabs[levels + lev]) for lev in range(levels)]
    values = [
        [metric * (across_diff(u) - belt_diff(v)) for u, v in pairs],
        [metric * (-belt_diff(u) - across_diff(v)) for u, v in pairs],
    ]
    values = diffused(values, [weights(kappas[c], closed) for c in range(2)])

    lane = lax.broadcasted_iota(jnp.int32, (rows, LANES), 1)
    lane_tile = lane[:SUB]
    low, high = MARGIN, LANES - MARGIN
    first_tile, last_tile = slice(0, LANES), slice(WINDOW - LANES, WINDOW)
    for c in range(2):
        for lev in range(levels):
            result, added = values[c][lev][:rows], grown_ref[c, lev]
            turned = pltpu.roll(result, LANES // 2, 1)
            head_ref[c, lev] = jnp.where(lane < low, pltpu.roll(result, LANES - SUB, 1), m0_ref[c, lev, :, first_tile])
            seam_ref[c, lev, :, :LANES] = jnp.where(lane >= high, turned, m0_ref[c, lev, :, last_tile])
            seam_ref[c, lev, :, LANES:] = jnp.where(lane < low, turned, m1_ref[c, lev, :, first_tile])
            tail_ref[c, lev] = jnp.where(lane >= high, pltpu.roll(result, SUB, 1), m1_ref[c, lev, :, last_tile])
            head_ref[c, lev, edge_rows] = head_ref[c, lev, edge_rows] + jnp.where(
                lane_tile >= low, added[:, first_tile], 0.0
            )
            seam_ref[c, lev, edge_rows, :LANES] = seam_ref[c, lev, edge_rows, :LANES] + jnp.where(
                lane_tile < high, added[:, last_tile], 0.0
            )
            strip_ref[c, lev] = m0_ref[c, lev, edge_rows, inner] + added[:, inner]
    late = [
        pltpu.make_async_copy(strip_ref, out_hbm.at[:, :, edge_rows, inner], sems.at[2]),
        pltpu.make_async_copy(head_ref, out_hbm.at[:, :, :, :LANES], sems.at[3]),
        pltpu.make_async_copy(seam_ref, out_hbm.at[:, :, :, WINDOW - LANES : WINDOW + LANES], sems.at[4]),
        pltpu.make_async_copy(tail_ref, out_hbm.at[:, :, :, cols - LANES :], sems.at[5]),
    ]
    for copy in late:
        copy.start()
    for copy in early + late:
        copy.wait()


def per_device(wind, metric, kappa, edge_peer, edge_flip, edge_turn):
    _, levels, rows, cols = wind.shape
    n_across, n_belt = lax.axis_size("across"), lax.axis_size("belt")
    halves = 1 if n_across == 2 else 2
    fields = 2 * levels
    bands = fields + 6
    corner_cols = LANES * (-(-bands // (2 * SLOTS)))
    side_cols = LANES * (-(-bands * (rows // SUB) // (2 * SLOTS)))
    ends_col = side_cols + corner_cols
    relay = halves == 1 and n_belt == 4 and ends_col + LANES <= cols

    vmem = pl.BlockSpec(memory_space=pltpu.VMEM)
    anywhere = pl.BlockSpec(memory_space=pl.ANY)
    lay = Rows(levels, rows, halves)
    height, span = lay.height, lay.span
    bulk, corner, rim, side, own, pick, facts = pl.pallas_call(
        functools.partial(pack_kernel, halves, ends_col if relay else None, n_belt),
        out_shape=[
            jax.ShapeDtypeStruct((halves, SUB * bands, cols), BF),
            jax.ShapeDtypeStruct((halves, 16, corner_cols), BF),
            jax.ShapeDtypeStruct((16, cols), BF),
            jax.ShapeDtypeStruct((16, cols), BF),
            jax.ShapeDtypeStruct((rows * bands, cols), BF),
            jax.ShapeDtypeStruct((16, cols), BF),
            jax.ShapeDtypeStruct((12, 16, LANES), F32),
        ],
        in_specs=[anywhere] * 6,
        out_specs=[vmem] * 7,
        scratch_shapes=[
            pltpu.VMEM(wind.shape, BF),
            pltpu.VMEM(kappa.shape, F32),
            pltpu.VMEM(metric.shape, F32),
            pltpu.SMEM(edge_peer.shape, jnp.int32),
            pltpu.SMEM(edge_flip.shape, jnp.int32),
            pltpu.SMEM(edge_turn.shape, jnp.int32),
            pltpu.SemaphoreType.DMA((6,)),
        ],
        compiler_params=pltpu.CompilerParams(vmem_limit_bytes=PACK_LIMIT),
        name="pack",
    )(
        *(
            pltpu.with_memory_space_constraint(x, pltpu.HBM)
            for x in (wind, metric, kappa, edge_peer, edge_flip, edge_turn)
        )
    )

    pairs_a = [(i, i ^ 1) for i in range(n_belt)]
    pairs_b = [(i, (i + 1) % n_belt if i % 2 else (i - 1) % n_belt) for i in range(n_belt)]
    if halves == 1:
        swap = [(0, 1), (1, 0)]
        bulk_in = lax.ppermute(bulk, "across", swap)
        corner_in = lax.ppermute(corner, "across", swap)
    else:
        onward = [(i, i + 1) for i in range(n_across - 1)]
        back = [(i + 1, i) for i in range(n_across - 1)]

        def both_ways(message):
            return jnp.stack(
                [
                    lax.ppermute(message[1], "across", back),
                    lax.ppermute(message[0], "across", onward),
                ]
            )

        corner_in, bulk_in = both_ways(corner), both_ways(bulk)
    bulk_in = bulk_in.reshape(halves, bands, SUB, cols).swapaxes(0, 1).reshape(bands * span, cols)

    def middle(k, messages):
        shapes = [jax.ShapeDtypeStruct((2, levels, rows, WINDOW), F32)]
        more = []
        operands = [own, bulk_in, *messages]
        spaces = [vmem] * len(operands)
        if k == 0:
            shapes += [
                jax.ShapeDtypeStruct((WINDOW, 2 * WINDOW), BF),
                jax.ShapeDtypeStruct((2, 5, PARTS, SUB, LANES), F32),
                jax.ShapeDtypeStruct((PARTS, SUB, LANES), F32),
            ]
        else:
            shapes += [
                jax.ShapeDtypeStruct((2, SUB, cols + LANES), F32),
                jax.ShapeDtypeStruct((2, levels, SUB, WINDOW), F32),
            ]
            if relay:
                more = [pltpu.VMEM((3, 16, cols), BF), pltpu.VMEM((4, 16, LANES), BF)]
        return pl.pallas_call(
            functools.partial(middle_kernel, lay, k, (side_cols, ends_col) if relay else None),
            out_shape=shapes,
            in_specs=spaces,
            out_specs=[vmem] * len(shapes),
            scratch_shapes=[pltpu.VMEM((height * bands + 2 * SUB * k, WINDOW), BF)]
            + work_shapes(lay, k)
            + more,
            compiler_params=pltpu.CompilerParams(vmem_limit_bytes=MID_LIMIT),
            cost_estimate=pl.CostEstimate(flops=2_000_000_000, bytes_accessed=2_000_000, transcendentals=0),
            name="middle",
        )(*operands)

    window_0, *shared = middle(0, [])
    if relay:
        spot = slice(side_cols, ends_col)
        side = jnp.concatenate([side[:, :side_cols], corner_in[0], side[:, ends_col:]], axis=1)
        far = lax.ppermute(jnp.concatenate([rim, side]), "belt", [(i, i ^ 2) for i in range(n_belt)])
        rim_c, side_c = far[:16], far[16:]
        chosen = jnp.where(pick > 0, rim, rim_c)
        near = lax.ppermute(jnp.concatenate([chosen, side, side_c]), "belt", pairs_a)
        rim_parts, messages = [rim, side, far, near], [near]
    else:
        side_a = lax.ppermute(side, "belt", pairs_a)
        side_b = lax.ppermute(side, "belt", pairs_b)
        corner_a = lax.ppermute(corner_in, "belt", pairs_a)
        corner_b = lax.ppermute(corner_in, "belt", pairs_b)
        rims = lax.all_gather(rim, "belt")
        if n_belt == 4:
            at_belt = lax.axis_index("belt")
            rims, ends = (rims[at_belt ^ jnp.array([0, 1, 2])], rims[at_belt ^ jnp.array([0, 1, 3, 2])])
        else:
            ends = rims
        ends = jnp.concatenate([ends[..., : LANES // 2], ends[..., cols - LANES // 2 :]], axis=-1)

        rim_parts, messages = [rims, ends], [side_a, side_b, corner_a, corner_b]
    window_1, ghost, grown = middle(1, [*shared, facts, *rim_parts])
    operands = [own, bulk_in, ghost, grown, window_0, window_1, *messages]
    return pl.pallas_call(
        functools.partial(edge_kernel, lay, (side_cols, ends_col) if relay else None),
        out_shape=jax.ShapeDtypeStruct((2, levels, rows, cols), F32),
        in_specs=[vmem] * len(operands),
        out_specs=anywhere,
        scratch_shapes=[
            pltpu.VMEM((2, levels, rows, LANES), F32),
            pltpu.VMEM((2, levels, rows, 2 * LANES), F32),
            pltpu.VMEM((2, levels, rows, LANES), F32),
            pltpu.VMEM((2, levels, SUB, WINDOW - 2 * LANES), F32),
            pltpu.SemaphoreType.DMA((6,)),
        ],
        compiler_params=pltpu.CompilerParams(vmem_limit_bytes=EDGE_LIMIT),
        name="edges",
    )(*operands)


def solution(mesh):
    return jax.shard_map(
        per_device,
        mesh=mesh,
        in_specs=(
            P(None, ("members", "lev"), "across", "belt"),
            P("across", "belt"),
            P(None, "across", "belt"),
            P(),
            P(),
            P(),
        ),
        out_specs=P(None, ("members", "lev"), "across", "belt"),
        check_vma=False,
    )
```

```python
import functools

import jax
import jax.numpy as jnp
import numpy as np
from jax import lax
from jax.experimental import pallas as pl
from jax.experimental.pallas import tpu as pltpu
from jax.sharding import PartitionSpec as P

STEPS = 6
LANES = 128
SUB = 8
SLOTS = 8
BF = jnp.bfloat16
F32 = jnp.float32
MARGIN = STEPS + 1
PARTS = 4
WINDOW = PARTS * LANES
PACK_LIMIT = 8 << 20
MID_LIMIT = 20 << 20
EDGE_LIMIT = 20 << 20


def split_hi_lo(value):
    hi = value.astype(BF).astype(F32)
    return hi, value - hi


def lane_iota():
    return lax.broadcasted_iota(jnp.int32, (SUB, LANES), 1)


def sub_iota(width):
    return lax.broadcasted_iota(jnp.int32, (SUB, width), 0)


def compact(tiles):
    slot = lane_iota() // 16
    packed = []
    for at in range(0, len(tiles), SLOTS):
        total = None
        for g, tile in enumerate(tiles[at : at + SLOTS]):
            moved = pltpu.roll(tile, (8 + 16 * g) % LANES, 1)
            total = moved if total is None else jnp.where(slot == g, moved, total)
        packed.append(total)
    return packed


def fetched(pairs, sems):
    copies = [pltpu.make_async_copy(src, dst, sems.at[i]) for i, (src, dst) in enumerate(pairs)]
    for copy in copies:
        copy.start()
    return copies


def edge_tile(band):
    left = lax.broadcasted_iota(jnp.int32, (band.shape[0], LANES), 1) < LANES // 2
    return jnp.where(left, band[:, :LANES], band[:, band.shape[1] - LANES :])


def compact_rows(tiles):
    packed = compact(tiles)
    packed += [jnp.zeros((SUB, LANES), F32)] * (-len(packed) % 2)
    return [jnp.concatenate(packed[i : i + 2], axis=0).astype(BF) for i in range(0, len(packed), 2)]


def pack_rows_kernel(halves, wind_hbm, metric_hbm, kappa_hbm, bulk_ref, corner_ref, *scratch):
    wind_ref, kappa_ref, metric_ref, sems = scratch
    levels, rows = wind_hbm.shape[1], wind_hbm.shape[2]
    first = lax.axis_index("across") == 0

    def load(slot, at):
        band = pl.multiple_of(jnp.where(at == 0, 0, rows - SUB), SUB)
        return [
            (wind_hbm.at[:, :, pl.ds(at, 16)], wind_ref.at[slot]),
            (kappa_hbm.at[:, pl.ds(band, SUB)], kappa_ref.at[slot]),
            (metric_hbm.at[pl.ds(band, SUB)], metric_ref.at[slot]),
        ]

    if halves == 1:
        spots = [pl.multiple_of(jnp.where(first, rows - 16, 0), 16)]
        low = [first]
    else:
        spots = [jnp.int32(rows - 16), jnp.int32(0)]
        low = [True, False]
    copies = fetched(sum([load(k, at) for k, at in enumerate(spots)], []), sems)
    for copy in copies:
        copy.wait()
    for k in range(halves):
        pieces = []
        for c in range(2):
            for lev in range(levels):
                both = wind_ref[k, c, lev].astype(F32)
                pieces.append(jnp.where(low[k], both[SUB:], both[:SUB]))
        for q in range(3):
            pieces += split_hi_lo(kappa_ref[k, q] if q < 2 else metric_ref[k])
        for i in range(0, len(pieces), 2):
            both = jnp.concatenate([pieces[i], pieces[i + 1]], axis=0)
            bulk_ref[k, SUB * i : SUB * (i + 2)] = both.astype(BF)
        for i, tile in enumerate(compact_rows([edge_tile(p) for p in pieces])):
            corner_ref[k, :, LANES * i : LANES * (i + 1)] = tile


def pack_kernel(
    ends_col, n_belt, wind_hbm, metric_hbm, kappa_hbm, peer_hbm, flip_hbm, turn_hbm,
    rim_ref, side_ref, own_ref, pick_ref, facts_ref, *scratch
):
    wind_ref, kappa_ref, metric_ref, peer_ref, flip_ref, turn_ref, sems = scratch
    levels, rows, cols = wind_hbm.shape[1:]
    first = lax.axis_index("across") == 0
    pairs = [(wind_hbm, wind_ref), (kappa_hbm, kappa_ref), (metric_hbm, metric_ref)]
    pairs += [(peer_hbm, peer_ref), (flip_hbm, flip_ref), (turn_hbm, turn_ref)]
    for copy in fetched(pairs, sems):
        copy.wait()
    at_belt = lax.axis_index("belt")
    edge = jnp.where(first, 0, 1)
    for i, block in enumerate((at_belt, lax.rem(at_belt + 1, n_belt), lax.rem(at_belt + n_belt - 1, n_belt))):
        slot = (end_slot if i else rim_slot)(peer_ref[edge, block], at_belt, n_belt)
        turn = turn_ref[edge, block]
        cosine = jnp.where(turn == 0, 1.0, jnp.where(turn == 2, -1.0, 0.0))
        sine_neg = jnp.where(turn == 1, -1.0, jnp.where(turn == 3, 1.0, 0.0))
        found = (slot.astype(F32), flip_ref[edge, block].astype(F32), cosine, sine_neg)
        for k, value in enumerate(found):
            facts_ref[4 * i + k] = jnp.full((16, LANES), value, F32)
    wanted = peer_ref[edge, at_belt ^ 1]
    pick_ref[...] = jnp.full(pick_ref.shape, jnp.where(wanted == at_belt, 1.0, 0.0), BF)
    tiles, rim_rows = [], []
    for f in range(2 * levels):
        own_ref[rows * f : rows * (f + 1)] = wind_ref[f // levels, f % levels]
        whole = wind_ref[f // levels, f % levels].astype(F32)
        tiles += [edge_tile(whole[r : r + SUB]) for r in range(0, rows, SUB)]
        rim_rows.append(jnp.where(first, whole[0:1], whole[rows - 1 : rows]))
    for q in range(3):
        for half, part in enumerate(split_hi_lo(kappa_ref[q] if q < 2 else metric_ref[...])):
            at = rows * (2 * levels + 2 * q + half)
            own_ref[at : at + rows] = part.astype(BF)
            tiles += [edge_tile(part[r : r + SUB]) for r in range(0, rows, SUB)]
    rim = jnp.concatenate(rim_rows + [jnp.zeros((16 - len(rim_rows), cols), F32)], axis=0)
    rim_ref[...] = rim.astype(BF)
    side_ref[...] = jnp.zeros(side_ref.shape, BF)
    for i, tile in enumerate(compact_rows(tiles)):
        side_ref[:, LANES * i : LANES * (i + 1)] = tile
    if ends_col is not None:
        side_ref[:, ends_col : ends_col + LANES] = edge_tile(rim).astype(BF)


def rim_slot(block, at_belt, n_belt):
    if n_belt != 4:
        return block
    return jnp.where(block == at_belt, 0, jnp.where((block ^ at_belt) == 2, 2, 1))


def end_slot(block, at_belt, n_belt):
    if n_belt != 4:
        return block
    offset = block ^ at_belt
    return jnp.where(offset == 2, 3, jnp.where(offset == 3, 2, offset))


class Rows:
    def __init__(self, levels, rows, halves):
        self.levels, self.rows, self.halves = levels, rows, halves
        self.fields, self.bands = 2 * levels, 2 * levels + 6
        self.tiles, self.span = rows // SUB, SUB * halves
        self.slab = self.tiles + halves
        self.height = SUB * self.slab

    def own_base(self, f):
        return 2 * self.height * (f // 2) + (self.height + self.span) * (f % 2)

    def band_base(self, f):
        return 2 * self.height * (f // 2) + self.rows

    def place_of(self, f, e):
        return e if f % 2 == 0 else (e + self.halves) % self.slab


def east_of(f):
    return [*f[1:], pltpu.roll(f[0], LANES - 1, 1)]


def west_of(f):
    return [pltpu.roll(f[-1], 1, 1), *f[:-1]]


def order_kernel(after_ref, order_ref):
    del after_ref
    fill_order(order_ref, 0)


def fill_order(order_ref, offset):
    size = order_ref.shape[0]
    at = lax.broadcasted_iota(jnp.int32, (size, LANES), 0)
    lane = lax.broadcasted_iota(jnp.int32, (1, LANES), 1)
    for r in range(PARTS):
        tile = jnp.where(at == PARTS * lane + (r + offset), 1.0, 0.0).astype(BF)
        order_ref[:, LANES * r : LANES * (r + 1)] = tile
        order_ref[:, LANES * (PARTS + r) : LANES * (PARTS + r + 1)] = tile


def solve_window(lay, first, last, x_ref, order_ref, work, extra=None):
    y_ref, coef_ref, met_ref, even_ref, odd_ref, fin_ref, z_ref = work
    levels, rows, fields, tiles = lay.levels, lay.rows, lay.fields, lay.tiles
    slab, height, span = lay.slab, lay.height, lay.span
    sub = lax.broadcasted_iota(jnp.int32, (SUB, LANES), 0)
    sub_slab = lax.broadcasted_iota(jnp.int32, (height, LANES), 0)
    closed = ((sub_slab == rows - 1) & last) | ((sub_slab == height - 1) & first)

    def put(ref, f, r, i, value):
        ref[f, r, SUB * (i + 1) : SUB * (i + 2)] = value
        if i == 0:
            ref[f, r, SUB * (slab + 1) : SUB * (slab + 2)] = value
        if i == slab - 1:
            ref[f, r, 0:SUB] = value
        if r == 0:
            return [(ref, f, PARTS, i, pltpu.roll(value, LANES - 1, 1))]
        if r == PARTS - 1:
            return [(ref, f, PARTS + 1, i, pltpu.roll(value, 1, 1))]
        return []

    def flush(rotated):
        for ref, f, plane, i, value in rotated:
            ref[f, plane, SUB * (i + 1) : SUB * (i + 2)] = value

    extra_place = slab + 2

    def advance(source, target, final):
        waiting = []
        for c in range(2):
            for e in [*range(tiles if final else slab)] + [None] * (extra is not None):
                mid, east, west, south, north = (
                    [
                        extra[0][c, k, r] if e is None else coef_ref[c, k, r, SUB * e : SUB * (e + 1)]
                        for r in range(PARTS)
                    ]
                    for k in range(5)
                )

                def place(f, e=e):
                    return extra_place if e is None else lay.place_of(f, e)

                results = []
                for lev in range(levels):
                    f = c * levels + lev
                    at = SUB * (place(f) + 1)
                    here = [source[f, r, at : at + SUB] for r in range(PARTS + 2)]
                    right = here[1 : PARTS + 1]
                    left = [here[PARTS + 1], *here[: PARTS - 1]]
                    results.append(
                        [
                            (mid[r] * here[r] + south[r] * source[f, r, at + 1 : at + 1 + SUB])
                            + north[r] * source[f, r, at - 1 : at - 1 + SUB]
                            + (east[r] * right[r] + west[r] * left[r])
                            for r in range(PARTS)
                        ]
                    )
                rotated = []
                for lev in range(levels):
                    f = c * levels + lev
                    for r in range(PARTS):
                        if final:
                            at = rows * fields + SUB * f if e is None else rows * f + SUB * e
                            fin_ref[at : at + SUB, LANES * r : LANES * (r + 1)] = results[lev][r]
                        else:
                            rotated += put(target, f, r, place(f), results[lev][r])
                flush(waiting)
                waiting = rotated
        flush(waiting)

    whole = jnp.dot(x_ref[...], order_ref[:, 0:WINDOW], preferred_element_type=F32)
    for r in range(PARTS):
        y_ref[r] = whole[:, LANES * r : LANES * (r + 1)]
    for q in range(3):
        base = height * (fields + 2 * q)
        low = base + height
        value = [
            y_ref[r, base : base + height]
            + jnp.concatenate([y_ref[r, low + span : low + height], y_ref[r, low : low + span]], axis=0)
            for r in range(PARTS)
        ]
        if q == 2:
            for r in range(PARTS):
                met_ref[r] = 0.5 * value[r]
            continue
        right = east_of(value)
        east = [0.5 * (value[r] + right[r]) for r in range(PARTS)]
        west = west_of(east)
        for r in range(PARTS):
            south = jnp.where(closed, 0.0, 0.5 * (value[r] + pltpu.roll(value[r], height - 1, 0)))
            north = pltpu.roll(south, 1, 0)
            coef_ref[q, 0, r] = 1.0 - ((east[r] + west[r]) + (south + north))
            coef_ref[q, 1, r] = east[r]
            coef_ref[q, 2, r] = west[r]
            coef_ref[q, 3, r] = south
            coef_ref[q, 4, r] = north
    waiting = []
    for e in range(slab):
        rotated = []
        metric = [met_ref[r, SUB * e : SUB * (e + 1)] for r in range(PARTS)]
        for lev in range(levels):
            across, belt = [], []
            for c in range(2):
                f = c * levels + lev
                base, i = height * f, lay.place_of(f, e)
                at = base + SUB * i
                here = [y_ref[r, at : at + SUB] for r in range(PARTS)]
                right, left = east_of(here), west_of(here)
                belt.append([right[r] - left[r] for r in range(PARTS)])
                diffs = []
                for r in range(PARTS):
                    if i < slab - 1:
                        below = y_ref[r, at + 1 : at + 1 + SUB]
                    else:
                        wrap = pltpu.roll(y_ref[r, base : base + SUB], SUB - 1, 0)
                        below = jnp.where(sub == SUB - 1, wrap, pltpu.roll(here[r], SUB - 1, 0))
                    if i > 0:
                        above = y_ref[r, at - 1 : at - 1 + SUB]
                    else:
                        end = base + height
                        wrap = pltpu.roll(y_ref[r, end - SUB : end], 1, 0)
                        above = jnp.where(sub == 0, wrap, pltpu.roll(here[r], 1, 0))
                    diffs.append(below - above)
                across.append(diffs)
            for r in range(PARTS):
                curl = metric[r] * (across[0][r] - belt[1][r])
                divergence = metric[r] * (-belt[0][r] - across[1][r])
                rotated += put(even_ref, lev, r, lay.place_of(lev, e), curl)
                rotated += put(even_ref, levels + lev, r, lay.place_of(levels + lev, e), divergence)
        flush(waiting)
        waiting = rotated
    flush(waiting)

    if extra is not None:
        for ref in (even_ref, odd_ref):
            for at in (extra_place, extra_place + 2):
                ref[:, 0:PARTS, SUB * at : SUB * (at + 1)] = jnp.zeros((fields, PARTS, SUB, LANES), F32)
        rotated = []
        for f in range(fields):
            c, lev = f // levels, f % levels
            at = height * lay.bands + SUB * c + lev
            for r in range(PARTS):
                value = (1.0 - 2.0 * c) * extra[1][r] * y_ref[r, at : at + 1]
                rotated += put(even_ref, f, r, extra_place, value)
        flush(rotated)

    def two(k, _):
        advance(even_ref, odd_ref, False)
        advance(odd_ref, even_ref, False)
        return 0

    lax.fori_loop(0, STEPS // 2 - 1, two, 0)
    advance(even_ref, odd_ref, False)
    advance(odd_ref, None, True)
    value = fin_ref[...]
    hi = value.astype(BF)
    z_ref[:, 0:WINDOW] = hi
    z_ref[:, WINDOW:] = (value - hi.astype(F32)).astype(BF)


def work_shapes(lay, extra):
    out_rows = (lay.rows + SUB * extra) * lay.fields
    plane = (lay.fields, PARTS + 2, lay.height + 2 * SUB + 3 * SUB * extra, LANES)
    return [
        pltpu.VMEM((PARTS, lay.height * lay.bands + 2 * SUB * extra, LANES), F32),
        pltpu.VMEM((2, 5, PARTS, lay.height, LANES), F32),
        pltpu.VMEM((PARTS, lay.height, LANES), F32),
        pltpu.VMEM(plane, F32),
        pltpu.VMEM(plane, F32),
        pltpu.VMEM((out_rows, WINDOW), F32),
        pltpu.VMEM((out_rows, 2 * WINDOW), BF),
    ]


def back_to_natural(z, order):
    return lax.dot_general(z, order, (((1,), (1,)), ((), ())), preferred_element_type=F32)


def ghost_tile_at(lay, first):
    return pl.multiple_of(jnp.where(first, 0, lay.rows - SUB), SUB)


def collect_rims(relay, refs, rims_ref, ends_ref):
    rim_ref, side_ref, far_ref, near_ref = refs
    for k, rim in enumerate((rim_ref[...], near_ref[0:16], far_ref[0:16])):
        rims_ref[k] = rim
    ends_cols = slice(relay[1], relay[1] + LANES)
    for k, (ref, at) in enumerate(((side_ref, 0), (near_ref, 16), (near_ref, 32), (far_ref, 16))):
        ends_ref[k] = ref[at : at + 16, ends_cols]


def ghost_rows(lay, facts_ref, rims_ref, ends_ref, ghost_ref):
    levels, cols = lay.levels, rims_ref.shape[-1]
    col_tiles = cols // LANES
    ghost_ref[...] = jnp.zeros(ghost_ref.shape, F32)

    def selected(i, ref, place):
        found = ref[0, :, place].astype(F32)
        for q in range(1, ref.shape[0]):
            found = jnp.where(facts_ref[4 * i] == q, ref[q, :, place].astype(F32), found)
        return found

    raw = [selected(0, rims_ref, slice(LANES * t, LANES * (t + 1))) for t in range(col_tiles)]
    raw += [selected(i, ends_ref, slice(0, LANES)) for i in (1, 2)]
    lane_r = lax.broadcasted_iota(jnp.int32, (LANES, LANES), 0)
    lane_c = lax.broadcasted_iota(jnp.int32, (LANES, LANES), 1)
    backward = jnp.where(lane_r + lane_c == LANES - 1, 1.0, 0.0).astype(BF)
    turned = reorder(jnp.concatenate(raw, axis=0).astype(BF), backward)

    def ghost_parts(i, plain, flipped):
        found = jnp.where(facts_ref[4 * i + 1] == 1, turned[16 * flipped : 16 * (flipped + 1)], raw[plain])
        p, q = found[0:levels], found[levels : 2 * levels]
        cosine, sine_neg = facts_ref[4 * i + 2, 0:levels], facts_ref[4 * i + 3, 0:levels]
        return cosine * p + sine_neg * q, cosine * q - sine_neg * p

    for t in range(col_tiles):
        for c, part in enumerate(ghost_parts(0, t, col_tiles - 1 - t)):
            ghost_ref[c, 0:levels, LANES * t : LANES * (t + 1)] = part
    after_tiles = ghost_parts(1, col_tiles, col_tiles)
    before_tiles = ghost_parts(2, col_tiles + 1, col_tiles + 1)
    lane_row = lax.broadcasted_iota(jnp.int32, (levels, LANES), 1)
    for c in range(2):
        both = jnp.where(lane_row < LANES // 2, after_tiles[c], before_tiles[c])
        ghost_ref[c, 0:levels, cols:] = both


def reorder(rows, order):
    return jnp.dot(rows, order, preferred_element_type=F32)


def middle_kernel(lay, k, relay, own_ref, bulk_ref, *rest):
    first, last = lax.axis_index("across") == 0, lax.axis_index("across") == lax.axis_size("across") - 1
    ghost_ref = None
    if k == 1:
        order_ref, weights_ref, touched_ref, facts_ref, *rest = rest
        if relay is None:
            rims_ref, ends_ref, out_ref, ghost_ref, grown_ref, x_ref, *work = rest
        else:
            *rest, rims_ref, ends_ref = rest
            collect_rims(relay, rest[:4], rims_ref, ends_ref)
            out_ref, ghost_ref, grown_ref, x_ref, *work = rest[4:]
        ghost_rows(lay, facts_ref, rims_ref, ends_ref, ghost_ref)
    else:
        order_ref, out_ref, weights_ref, touched_ref, x_ref, *work = rest
    cols = slice(WINDOW * k, WINDOW * (k + 1))
    for f in range(lay.bands):
        base = lay.own_base(f)
        x_ref[base : base + lay.rows] = own_ref[lay.rows * f : lay.rows * (f + 1), cols]
    span = lay.span
    at_row = lax.broadcasted_iota(jnp.int32, (2 * span, WINDOW), 0)
    for f in range(0, lay.bands, 2):
        band = bulk_ref[span * f : span * (f + 2), cols]
        if f < lay.fields:
            band = band.astype(F32)
            for g in range(2):
                c, lev = (f + g) // lay.levels, (f + g) % lay.levels
                row = 0.0 if ghost_ref is None else ghost_ref[c, lev : lev + 1, cols]
                spot = jnp.where(first, span * (g + 1) - 1, jnp.where(last, span * g, -1))
                band = jnp.where(at_row == spot, row, band)
            band = band.astype(BF)
        at = lay.band_base(f)
        x_ref[at : at + 2 * span] = band
    extra = None
    if k == 1:
        beside = jnp.concatenate([ghost_ref[c, :, :WINDOW] for c in range(2)], axis=0)
        x_ref[lay.height * lay.bands :] = beside.astype(BF)
        sub = lax.broadcasted_iota(jnp.int32, (SUB, LANES), 0)
        sign = jnp.where(first, -1.0, jnp.where(last, 1.0, 0.0))
        lift = jnp.where(sub == jnp.where(first, 0, SUB - 1), sign, 0.0)
        extra = weights_ref, [lift * touched_ref[r] for r in range(PARTS)]
    solve_window(lay, first, last, x_ref, order_ref, work, extra)
    back = back_to_natural(work[-1][...], order_ref[...])
    for f in range(lay.fields):
        c, lev = f // lay.levels, f % lay.levels
        out_ref[c, lev] = back[lay.rows * f : lay.rows * (f + 1)]
        if k == 1:
            at = lay.rows * lay.fields + SUB * f
            grown_ref[c, lev] = back[at : at + SUB]
    if k == 0:
        at = ghost_tile_at(lay, first)
        weights_ref[...] = work[1][:, :, :, pl.ds(at, SUB)]
        touched_ref[...] = work[2][:, pl.ds(at, SUB)]


def weights(kappa, closed_rows):
    height, width = kappa.shape
    east = 0.5 * (kappa + pltpu.roll(kappa, width - 1, 1))
    west = pltpu.roll(east, 1, 1)
    south = jnp.where(closed_rows, 0.0, 0.5 * (kappa + pltpu.roll(kappa, height - 1, 0)))
    north = pltpu.roll(south, 1, 0)
    return 1.0 - ((east + west) + (south + north)), east, west, south, north


def diffused(values, coefs):
    def step(f, mid, east, west, south, north):
        height, width = f.shape
        return (mid * f + east * pltpu.roll(f, width - 1, 1) + west * pltpu.roll(f, 1, 1)) + (
            south * pltpu.roll(f, height - 1, 0) + north * pltpu.roll(f, 1, 0)
        )

    for _ in range(STEPS):
        values = [[step(f, *coef) for f in component] for component, coef in zip(values, coefs)]
    return values


def edge_kernel(lay, relay, own_ref, bulk_ref, ghost_ref, grown_ref, m0_ref, m1_ref, *rest):
    if relay is None:
        side_a_ref, side_b_ref, corner_a_ref, corner_b_ref, *rest = rest
    else:
        near_ref, *rest = rest
        side_a_ref, side_b_ref = near_ref.at[16:32], near_ref.at[32:48]
        corner_a_ref, corner_b_ref = (near_ref.at[pl.ds(k, 16), relay[0] : relay[1]] for k in (16, 32))
    out_hbm, head_ref, seam_ref, tail_ref, strip_ref, sems = rest
    levels, rows, cols = lay.levels, lay.rows, own_ref.shape[1]
    tiles, halves, fields, bands, span = lay.tiles, lay.halves, lay.fields, lay.bands, lay.span
    at_belt, at_across = lax.axis_index("belt"), lax.axis_index("across")
    first, last = at_across == 0, at_across == lax.axis_size("across") - 1
    ghost_at = ghost_tile_at(lay, first)
    edge_rows = pl.ds(ghost_at, SUB)
    calm = pl.ds(pl.multiple_of(jnp.where(first, SUB, 0), SUB), rows - SUB)
    inner, after = slice(LANES, WINDOW - LANES), slice(WINDOW + LANES, cols - LANES)
    early = [
        pltpu.make_async_copy(m0_ref.at[:, :, calm, inner], out_hbm.at[:, :, calm, inner], sems.at[0]),
        pltpu.make_async_copy(m1_ref.at[:, :, :, inner], out_hbm.at[:, :, :, after], sems.at[1]),
        pltpu.make_async_copy(strip_ref, out_hbm.at[:, :, edge_rows, inner], sems.at[2]),
    ]
    strip_ref[...] = m0_ref[:, :, edge_rows, inner] + grown_ref[:, :, :, inner]
    for copy in early:
        copy.start()
    even = lax.rem(at_belt, 2) == 0
    from_right = (lane_iota() // 8) % 2 == 1
    take_a = from_right == even

    def unpacked(a_ref, b_ref, groups):
        out = []
        for g in range(groups):
            column, half = LANES * (g // 2), slice(SUB * (g % 2), SUB * (g % 2) + SUB)
            a = a_ref(column).astype(F32)[half]
            b = b_ref(column).astype(F32)[half]
            out.append(jnp.where(take_a, a, b))
        return out

    def put_back(packed, index):
        return pltpu.roll(packed[index // SLOTS], (-(8 + 16 * (index % SLOTS))) % LANES, 1)

    side_tiles = unpacked(
        lambda k: side_a_ref[:, k : k + LANES], lambda k: side_b_ref[:, k : k + LANES],
        -(-bands * tiles // SLOTS),
    )
    corners = [
        unpacked(
            lambda k, at=at: (corner_a_ref if relay else corner_a_ref.at[at])[:, k : k + LANES],
            lambda k, at=at: (corner_b_ref if relay else corner_b_ref.at[at])[:, k : k + LANES],
            -(-bands // SLOTS),
        )
        for at in range(halves)
    ]

    places = [slice(at, at + LANES) for at in (0, WINDOW - LANES, WINDOW, cols - LANES)]

    def fold(rows_of, halo):
        lane = lax.broadcasted_iota(jnp.int32, halo.shape, 1)
        start, before_seam, after_seam, end = (rows_of(place) for place in places)
        left = pltpu.roll(jnp.where(lane >= LANES - SUB, halo, start), SUB, 1)
        seam = pltpu.roll(jnp.where(lane >= LANES // 2, before_seam, after_seam), LANES // 2, 1)
        right = pltpu.roll(jnp.where(lane < SUB, halo, end), LANES - SUB, 1)
        return jnp.where(lane < 40, left, jnp.where(lane < 88, seam, right))

    ghosts = [fold(lambda place, c=c: ghost_ref[c, :, place], ghost_ref[c, :, cols:]) for c in range(2)]
    at_band = lax.broadcasted_iota(jnp.int32, (span, LANES), 0)
    spot = jnp.where(first, span - 1, jnp.where(last, 0, -1))
    slabs = []
    for f in range(bands):
        own = slice(rows * f, rows * (f + 1))
        halo = jnp.concatenate([put_back(side_tiles, f * tiles + r) for r in range(tiles)], axis=0)
        own_rows = fold(lambda place, own=own: own_ref[own, place].astype(F32), halo)
        pair, half = slice(span * (f - f % 2), span * (f - f % 2 + 2)), slice(span * (f % 2), span * (f % 2 + 1))
        band = fold(
            lambda place, pair=pair, half=half: bulk_ref[pair, place].astype(F32)[half],
            jnp.concatenate([put_back(corners[at], f) for at in range(halves)], axis=0),
        )
        if f < fields:
            c, lev = f // levels, f % levels
            band = jnp.where(at_band == spot, ghosts[c][lev : lev + 1], band)
        slabs.append(jnp.concatenate([own_rows, band], axis=0))
    at_row = lax.broadcasted_iota(jnp.int32, (lay.height, LANES), 0)
    closed = ((at_row == rows - 1) & last) | ((at_row == lay.height - 1) & first)
    kappas = [slabs[fields + 2 * q] + slabs[fields + 2 * q + 1] for q in range(3)]
    metric = 0.5 * kappas[2]

    def across_diff(f):
        return pltpu.roll(f, lay.height - 1, 0) - pltpu.roll(f, 1, 0)

    def belt_diff(f):
        return pltpu.roll(f, LANES - 1, 1) - pltpu.roll(f, 1, 1)

    pairs = [(slabs[lev], slabs[levels + lev]) for lev in range(levels)]
    values = [
        [metric * (across_diff(u) - belt_diff(v)) for u, v in pairs],
        [metric * (-belt_diff(u) - across_diff(v)) for u, v in pairs],
    ]
    values = diffused(values, [weights(kappas[c], closed) for c in range(2)])

    lane = lax.broadcasted_iota(jnp.int32, (rows, LANES), 1)
    lane_tile = lane[:SUB]
    low, high = MARGIN, LANES - MARGIN
    first_tile, last_tile = slice(0, LANES), slice(WINDOW - LANES, WINDOW)
    late = []
    for c in range(2):
        for lev in range(levels):
            result, added = values[c][lev][:rows], grown_ref[c, lev]
            turned = pltpu.roll(result, LANES // 2, 1)
            head_ref[c, lev] = jnp.where(lane < low, pltpu.roll(result, LANES - SUB, 1), m0_ref[c, lev, :, first_tile])
            seam_ref[c, lev, :, :LANES] = jnp.where(lane >= high, turned, m0_ref[c, lev, :, last_tile])
            seam_ref[c, lev, :, LANES:] = jnp.where(lane < low, turned, m1_ref[c, lev, :, first_tile])
            tail_ref[c, lev] = jnp.where(lane >= high, pltpu.roll(result, SUB, 1), m1_ref[c, lev, :, last_tile])
            head_ref[c, lev, edge_rows] = head_ref[c, lev, edge_rows] + jnp.where(
                lane_tile >= low, added[:, first_tile], 0.0
            )
            seam_ref[c, lev, edge_rows, :LANES] = seam_ref[c, lev, edge_rows, :LANES] + jnp.where(
                lane_tile < high, added[:, last_tile], 0.0
            )
        late += [
            pltpu.make_async_copy(ref.at[c], out_hbm.at[c, :, :, place], sems.at[3 + 3 * c + k])
            for k, (ref, place) in enumerate(
                (
                    (head_ref, slice(0, LANES)),
                    (seam_ref, slice(WINDOW - LANES, WINDOW + LANES)),
                    (tail_ref, slice(cols - LANES, cols)),
                )
            )
        ]
        for copy in late[3 * c :]:
            copy.start()
    for copy in early + late:
        copy.wait()


def per_device(wind, metric, kappa, edge_peer, edge_flip, edge_turn):
    _, levels, rows, cols = wind.shape
    n_across, n_belt = lax.axis_size("across"), lax.axis_size("belt")
    halves = 1 if n_across == 2 else 2
    fields = 2 * levels
    bands = fields + 6
    corner_cols = LANES * (-(-bands // (2 * SLOTS)))
    side_cols = LANES * (-(-bands * (rows // SUB) // (2 * SLOTS)))
    ends_col = side_cols + corner_cols
    relay = halves == 1 and n_belt == 4 and ends_col + LANES <= cols

    vmem = pl.BlockSpec(memory_space=pltpu.VMEM)
    anywhere = pl.BlockSpec(memory_space=pl.ANY)
    lay = Rows(levels, rows, halves)
    height, span = lay.height, lay.span
    pinned = [
        pltpu.with_memory_space_constraint(x, pltpu.HBM)
        for x in (wind, metric, kappa, edge_peer, edge_flip, edge_turn)
    ]
    bulk, corner = pl.pallas_call(
        functools.partial(pack_rows_kernel, halves),
        out_shape=[
            jax.ShapeDtypeStruct((halves, SUB * bands, cols), BF),
            jax.ShapeDtypeStruct((halves, 16, corner_cols), BF),
        ],
        in_specs=[anywhere] * 3,
        out_specs=[vmem] * 2,
        scratch_shapes=[
            pltpu.VMEM((halves, 2, levels, 16, cols), BF),
            pltpu.VMEM((halves, 2, SUB, cols), F32),
            pltpu.VMEM((halves, SUB, cols), F32),
            pltpu.SemaphoreType.DMA((3 * halves,)),
        ],
        compiler_params=pltpu.CompilerParams(vmem_limit_bytes=PACK_LIMIT),
        name="pack_rows",
    )(*pinned[:3])
    rim, side, own, pick, facts = pl.pallas_call(
        functools.partial(pack_kernel, ends_col if relay else None, n_belt),
        out_shape=[
            jax.ShapeDtypeStruct((16, cols), BF),
            jax.ShapeDtypeStruct((16, cols), BF),
            jax.ShapeDtypeStruct((rows * bands, cols), BF),
            jax.ShapeDtypeStruct((16, cols), BF),
            jax.ShapeDtypeStruct((12, 16, LANES), F32),
        ],
        in_specs=[anywhere] * 6,
        out_specs=[vmem] * 5,
        scratch_shapes=[
            pltpu.VMEM(wind.shape, BF),
            pltpu.VMEM(kappa.shape, F32),
            pltpu.VMEM(metric.shape, F32),
            pltpu.SMEM(edge_peer.shape, jnp.int32),
            pltpu.SMEM(edge_flip.shape, jnp.int32),
            pltpu.SMEM(edge_turn.shape, jnp.int32),
            pltpu.SemaphoreType.DMA((6,)),
        ],
        compiler_params=pltpu.CompilerParams(vmem_limit_bytes=PACK_LIMIT),
        name="pack",
    )(*pinned)

    pairs_a = [(i, i ^ 1) for i in range(n_belt)]
    pairs_b = [(i, (i + 1) % n_belt if i % 2 else (i - 1) % n_belt) for i in range(n_belt)]
    if halves == 1:
        swap = [(0, 1), (1, 0)]
        bulk_in = lax.ppermute(bulk, "across", swap)
        corner_in = lax.ppermute(corner, "across", swap)
    else:
        onward = [(i, i + 1) for i in range(n_across - 1)]
        back = [(i + 1, i) for i in range(n_across - 1)]

        def both_ways(message):
            return jnp.stack(
                [
                    lax.ppermute(message[1], "across", back),
                    lax.ppermute(message[0], "across", onward),
                ]
            )

        corner_in, bulk_in = both_ways(corner), both_ways(bulk)
    bulk_in = bulk_in.reshape(halves, bands, SUB, cols).swapaxes(0, 1).reshape(bands * span, cols)

    def middle(k, messages):
        shapes = [jax.ShapeDtypeStruct((2, levels, rows, WINDOW), F32)]
        more = []
        operands = [own, bulk_in, *messages]
        spaces = [vmem] * len(operands)
        if k == 0:
            shapes += [
                jax.ShapeDtypeStruct((2, 5, PARTS, SUB, LANES), F32),
                jax.ShapeDtypeStruct((PARTS, SUB, LANES), F32),
            ]
        else:
            shapes += [
                jax.ShapeDtypeStruct((2, SUB, cols + LANES), F32),
                jax.ShapeDtypeStruct((2, levels, SUB, WINDOW), F32),
            ]
            if relay:
                more = [pltpu.VMEM((3, 16, cols), BF), pltpu.VMEM((4, 16, LANES), BF)]
        return pl.pallas_call(
            functools.partial(middle_kernel, lay, k, (side_cols, ends_col) if relay else None),
            out_shape=shapes,
            in_specs=spaces,
            out_specs=[vmem] * len(shapes),
            scratch_shapes=[pltpu.VMEM((height * bands + 2 * SUB * k, WINDOW), BF)]
            + work_shapes(lay, k)
            + more,
            compiler_params=pltpu.CompilerParams(vmem_limit_bytes=MID_LIMIT),
            cost_estimate=pl.CostEstimate(flops=2_000_000_000, bytes_accessed=2_000_000, transcendentals=0),
            name="middle",
        )(*operands)

    def order_after(message):
        return pl.pallas_call(
            order_kernel,
            out_shape=jax.ShapeDtypeStruct((WINDOW, 2 * WINDOW), BF),
            in_specs=[anywhere],
            out_specs=vmem,
            compiler_params=pltpu.CompilerParams(vmem_limit_bytes=PACK_LIMIT),
            cost_estimate=pl.CostEstimate(flops=100_000_000, bytes_accessed=1_000_000, transcendentals=0),
            name="order",
        )(message)

    order = order_after(corner_in)
    window_0, *shared = middle(0, [order])
    if relay:
        spot = slice(side_cols, ends_col)
        side = jnp.concatenate([side[:, :side_cols], corner_in[0], side[:, ends_col:]], axis=1)
        far = lax.ppermute(jnp.concatenate([rim, side]), "belt", [(i, i ^ 2) for i in range(n_belt)])
        rim_c, side_c = far[:16], far[16:]
        chosen = jnp.where(pick > 0, rim, rim_c)
        near = lax.ppermute(jnp.concatenate([chosen, side, side_c]), "belt", pairs_a)
        rim_parts, messages = [rim, side, far, near], [near]
    else:
        side_a = lax.ppermute(side, "belt", pairs_a)
        side_b = lax.ppermute(side, "belt", pairs_b)
        corner_a = lax.ppermute(corner_in, "belt", pairs_a)
        corner_b = lax.ppermute(corner_in, "belt", pairs_b)
        rims = lax.all_gather(rim, "belt")
        if n_belt == 4:
            at_belt = lax.axis_index("belt")
            rims, ends = (rims[at_belt ^ jnp.array([0, 1, 2])], rims[at_belt ^ jnp.array([0, 1, 3, 2])])
        else:
            ends = rims
        ends = jnp.concatenate([ends[..., : LANES // 2], ends[..., cols - LANES // 2 :]], axis=-1)

        rim_parts, messages = [rims, ends], [side_a, side_b, corner_a, corner_b]
    window_1, ghost, grown = middle(1, [order, *shared, facts, *rim_parts])
    operands = [own, bulk_in, ghost, grown, window_0, window_1, *messages]
    return pl.pallas_call(
        functools.partial(edge_kernel, lay, (side_cols, ends_col) if relay else None),
        out_shape=jax.ShapeDtypeStruct((2, levels, rows, cols), F32),
        in_specs=[vmem] * len(operands),
        out_specs=anywhere,
        scratch_shapes=[
            pltpu.VMEM((2, levels, rows, LANES), F32),
            pltpu.VMEM((2, levels, rows, 2 * LANES), F32),
            pltpu.VMEM((2, levels, rows, LANES), F32),
            pltpu.VMEM((2, levels, SUB, WINDOW - 2 * LANES), F32),
            pltpu.SemaphoreType.DMA((9,)),
        ],
        compiler_params=pltpu.CompilerParams(vmem_limit_bytes=EDGE_LIMIT),
        name="edges",
    )(*operands)


def solution(mesh):
    return jax.shard_map(
        per_device,
        mesh=mesh,
        in_specs=(
            P(None, ("members", "lev"), "across", "belt"),
            P("across", "belt"),
            P(None, "across", "belt"),
            P(),
            P(),
            P(),
        ),
        out_specs=P(None, ("members", "lev"), "across", "belt"),
        check_vma=False,
    )
```
